32 devices in a mesh: groups: 2 (over y), space: 4 (over z), tangent: 4 (over x, core).
Axes of the slice: x: 2, y: 2, z: 4, core: 2. Of those that a mesh axis runs over, the one named last changes fastest.
Arguments:
- positions: float32 [16, 2, 128], P(('groups', 'space')), parts along dimension 0, may hold values from 0.45 to 15.55, as said below
- momenta: float32 [16, 2, 128], P(('groups', 'space')), parts along dimension 0, may hold values from -4 to 4
- cell_count: int32 [16], P(('groups', 'space')), parts along dimension 0, may hold values from 64 to 128, as said below
- tangent: float32 [16, 4, 128, 1024], P(('groups', 'space'), None, None, 'tangent'), parts along dimension 0, may hold values from -6 to 6
Outputs:
- phase: float32 [16, 4, 128], P(('groups', 'space')), parts along dimension 0
- new_tangent: float32 [16, 4, 128, 1024], P(('groups', 'space'), None, None, 'tangent'), parts along dimension 0
- stretch: float32 [2048], P(('groups', 'tangent')), parts along dimension 0
The draws below stay inside these ranges and needn't reach their ends.
There are 2 independent parts, one for each index of `groups`. The reference program is written for one: setup_inputs(seed, part) draws one part's arguments, and reference() takes and returns one part's arrays. A program takes and returns all parts, laid end to end along the dimension named above; each array names one. Nothing has to cross between parts.
Inputs may be any that keep to these rules, and one draw needn't show every extreme that they name: Slots 0 to cell_count - 1 of a cell hold particles, the others are padding; some cell holds 128 particles in every draw. `positions`: every slot of a cell, padding too, lies within 0.05 in each coordinate of its own point of the lattice (m + 0.5, n + 0.5), m from 0 to 7, n from 0 to 15; no two slots of a cell share a lattice point.
All inputs are finite; a program needn't handle non-finite values.
Results may differ from the reference program's by a relative error of at most 0.006.
Values may be sent and summed in bfloat16 or wider, within the bound.
No kernel may reach another device: no remote copies, remote signals or barrier semaphores. Data moves between devices by JAX's collectives and lax.ppermute only.
A program may use at most 128 MiB of HBM per device.

```python
import jax
import jax.numpy as jnp
from jax import lax

VECTORS = 1024
SLOTS = 128
CY = 2
STEPS = 2
NCELLS = 8
N_SPACE = 4


def draw_positions(key, part):
    keys = jax.random.split(jax.random.fold_in(key, 11), NCELLS)
    sites = jax.vmap(lambda single: jax.random.permutation(single, SLOTS))(keys)
    column = (sites % 8).astype(jnp.float32) + 0.5
    row_pos = (sites // 8).astype(jnp.float32) + 0.5
    lattice = jnp.stack([column, row_pos], axis=1)
    jitter = 0.025 * jnp.clip(jax.random.normal(jax.random.fold_in(key, 12), (NCELLS, 2, SLOTS), jnp.float32), -2.0, 2.0)
    return lattice + jitter


def draw_cell_count(key, part):
    base = jax.random.randint(jax.random.fold_in(key, 21), (NCELLS,), SLOTS // 2, SLOTS + 1)
    chosen = jax.random.randint(jax.random.fold_in(key, 22), (), 0, NCELLS)
    return jnp.where(jnp.arange(NCELLS, dtype=jnp.int32) == chosen, SLOTS, base).astype(jnp.int32)


def spiked(entries, rng, source, target, shards_of, factor):
    owner, partner = [(jnp.arange(entries.shape[position]) // (entries.shape[position] // shards_of)).reshape([-1 if axis == position else 1 for axis in range(entries.ndim)]) for position in (source, target)]
    chosen = jax.random.permutation(rng, shards_of)[partner]
    strong = (owner == chosen) | (owner == (partner + shards_of // 2) % shards_of)
    return jnp.where(strong, factor * entries, entries)


def level_of(key, dims, cuts, least, high):
    gain, own = 1.0, jax.random.fold_in(key, 6)
    for dim, parts in cuts:
        heights = jnp.exp(jax.random.uniform(jax.random.fold_in(own, dim), (parts,), jnp.float32, least / len(cuts), high / len(cuts)))
        gain = gain * jnp.repeat(heights, dims[dim] // parts).reshape([-1 if axis == dim else 1 for axis in range(len(dims))])
    return gain


def centred(rng, extent, scale, most, shards=(), kind=jnp.bfloat16):
    values = scale * jax.random.normal(rng, extent, jnp.float32)
    if shards:
        values = values * level_of(rng, extent, shards, -0.22, 0.18)
    return jnp.clip(values, -most, most).astype(kind)


def heavy_noise(stream_key, dims, deviation, most, pieces, heavy, held_as=jnp.bfloat16):
    result = deviation * jax.random.normal(stream_key, dims, jnp.float32)
    if pieces:
        result = result * level_of(stream_key, dims, pieces, -0.22, 0.18)
    return jnp.clip(spiked(result, jax.random.fold_in(stream_key, 3), *heavy), -most, most).astype(held_as)


def setup_inputs(seed: int = 0, part: int = 0) -> dict:
    splits = jax.random.split(jax.random.key(seed), 5)
    part_splits = jax.random.split(jax.random.fold_in(splits[4], part), 5)
    positions = draw_positions(jax.random.fold_in(jax.random.fold_in(splits[4], part), 71), part)
    momenta = centred(part_splits[1], (NCELLS, 2, SLOTS), 1.0, 4.0, ((0, 4),), jnp.float32)
    cell_count = draw_cell_count(jax.random.fold_in(jax.random.fold_in(splits[4], part), 71), part)
    tangent = heavy_noise(part_splits[3], (NCELLS, 4, SLOTS, VECTORS), 1.0, 6.0, ((0, 4), (3, 4)), (0, 3, 4, 2.0), jnp.float32)
    return {"positions": positions, "momenta": momenta, "cell_count": cell_count, "tangent": tangent}


DT = 0.005
CUT2 = 2.0 ** (1.0 / 3.0)
PARK = 1000.0
HIGH = lax.Precision.HIGHEST

def pair_terms(own_coords, own_alive, far_coords, shift_x, shift_y, same_cell):
    delta_x = shift_x + far_coords[..., 0, None, :] - own_coords[..., 0, :, None]
    delta_y = shift_y + far_coords[..., 1, None, :] - own_coords[..., 1, :, None]
    dist2 = delta_x * delta_x + delta_y * delta_y
    within = jnp.logical_and(dist2 < CUT2, own_alive[..., :, None] > 0.5)
    if same_cell:
        within = jnp.logical_and(within, jnp.logical_not(jnp.eye(dist2.shape[-1], dtype=bool)))
    weight = within.astype(jnp.float32)
    safe = jnp.where(within, dist2, CUT2)
    inverse = 1.0 / safe
    inv_three = inverse * inverse * inverse
    inv_six = inv_three * inv_three
    energy = 4.0 * (inv_six - inv_three) + 1.0
    energy_1 = 4.0 * (3.0 * inv_three - 6.0 * inv_six) * inverse
    energy_2 = 4.0 * (42.0 * inv_six - 12.0 * inv_three) * inverse * inverse
    taper = 1.0 - safe / CUT2
    switch = taper * taper
    switch_1 = -2.0 * taper / CUT2
    switch_2 = 2.0 / (CUT2 * CUT2)
    grad_1 = (energy_1 * switch + energy * switch_1) * weight
    grad_2 = (energy_2 * switch + 2.0 * energy_1 * switch_1 + energy * switch_2) * weight
    force_x = jnp.sum(2.0 * grad_1 * delta_x, axis=-1)
    force_y = jnp.sum(2.0 * grad_1 * delta_y, axis=-1)
    k_xx = (2.0 * grad_1 + 4.0 * grad_2 * delta_x * delta_x).astype(jnp.bfloat16)
    k_xy = (4.0 * grad_2 * delta_x * delta_y).astype(jnp.bfloat16)
    k_yy = (2.0 * grad_1 + 4.0 * grad_2 * delta_y * delta_y).astype(jnp.bfloat16)
    k_xx = lax.optimization_barrier(k_xx).astype(jnp.float32)
    k_xy = lax.optimization_barrier(k_xy).astype(jnp.float32)
    k_yy = lax.optimization_barrier(k_yy).astype(jnp.float32)
    return (force_x, force_y, k_xx, k_xy, k_yy)

def evaluate(coords, occupied, small_q):
    low = lax.optimization_barrier(small_q.astype(jnp.bfloat16)).astype(jnp.float32)
    parked = jnp.concatenate([coords[:, :, 0:1] + PARK * (1.0 - occupied)[:, :, None, :], coords[:, :, 1:2]], axis=2)
    forces_x = jnp.zeros(occupied.shape, jnp.float32)
    forces_y = jnp.zeros(occupied.shape, jnp.float32)
    push_x = jnp.zeros(low[:, :, 0].shape, jnp.float32)
    push_y = jnp.zeros(low[:, :, 0].shape, jnp.float32)
    diag_xx = jnp.zeros(occupied.shape, jnp.float32)
    diag_xy = jnp.zeros(occupied.shape, jnp.float32)
    diag_yy = jnp.zeros(occupied.shape, jnp.float32)
    for side in (-1, 0, 1):
        for lane in (-1, 0, 1):
            far_coords = jnp.roll(parked, (-side, -lane), axis=(0, 1))
            far_low = jnp.roll(low, (-side, -lane), axis=(0, 1))
            force_x, force_y, k_xx, k_xy, k_yy = pair_terms(parked, occupied, far_coords, 8.0 * side, 16.0 * lane, side == 0 and lane == 0)
            forces_x = forces_x + force_x
            forces_y = forces_y + force_y
            push_x = push_x + jnp.einsum('abij,abjv->abiv', k_xx, far_low[:, :, 0], precision=HIGH) + jnp.einsum('abij,abjv->abiv', k_xy, far_low[:, :, 1], precision=HIGH)
            push_y = push_y + jnp.einsum('abij,abjv->abiv', k_xy, far_low[:, :, 0], precision=HIGH) + jnp.einsum('abij,abjv->abiv', k_yy, far_low[:, :, 1], precision=HIGH)
            diag_xx = diag_xx + jnp.sum(k_xx, axis=-1)
            diag_xy = diag_xy + jnp.sum(k_xy, axis=-1)
            diag_yy = diag_yy + jnp.sum(k_yy, axis=-1)
    push_x = push_x - diag_xx[..., None] * low[:, :, 0] - diag_xy[..., None] * low[:, :, 1]
    push_y = push_y - diag_xy[..., None] * low[:, :, 0] - diag_yy[..., None] * low[:, :, 1]
    return (jnp.stack([forces_x, forces_y], axis=2), jnp.stack([push_x, push_y], axis=2))

def reference(positions, momenta, cell_count, tangent):
    occupied = (jnp.arange(SLOTS, dtype=jnp.int32)[None, :] < cell_count[:, None]).astype(jnp.float32)
    state = tangent * occupied[:, None, :, None]
    grid_shape = (N_SPACE, CY)
    occupied = occupied.reshape(grid_shape + (SLOTS,))
    coords = positions.reshape(grid_shape + (2, SLOTS))
    speeds = momenta.reshape(grid_shape + (2, SLOTS))
    state = state.reshape(grid_shape + (4, SLOTS, VECTORS))
    small_q = state[:, :, 0:2]
    small_p = state[:, :, 2:4]
    forces, pushes = evaluate(coords, occupied, small_q)
    for step_index in range(STEPS):
        midway_p = speeds + 0.5 * DT * forces
        midway_dp = small_p + 0.5 * DT * pushes
        coords = coords + DT * midway_p
        small_q = small_q + DT * midway_dp
        forces, pushes = evaluate(coords, occupied, small_q)
        speeds = midway_p + 0.5 * DT * forces
        small_p = midway_dp + 0.5 * DT * pushes
    phase = jnp.concatenate([coords, speeds], axis=2).reshape(NCELLS, 4, SLOTS)
    final = jnp.concatenate([small_q, small_p], axis=2).reshape(NCELLS, 4, SLOTS, VECTORS)
    flat_rows = final.reshape(-1, VECTORS)
    gram = jnp.dot(flat_rows.T.astype(jnp.float32), flat_rows.astype(jnp.float32), precision=HIGH, preferred_element_type=jnp.float32)
    gram = gram / (4.0 * SLOTS * NCELLS)
    factor = jnp.linalg.cholesky(gram)
    solved = jax.scipy.linalg.solve_triangular(factor, flat_rows.T, lower=True).T
    new_tangent = solved.reshape(NCELLS, 4, SLOTS, VECTORS)
    stretch = jnp.log(jnp.diagonal(factor))
    return (phase, new_tangent, stretch)
```

```python
import jax
import jax.numpy as jnp
from jax import lax
from jax.experimental import pallas as pl
from jax.experimental.pallas import tpu as pltpu
from jax.sharding import PartitionSpec as P

STEPS = 2


DT = 0.005
CUT2 = 2.0 ** (1.0 / 3.0)
PARK = 1000.0
HIGH = lax.Precision.HIGHEST


def padded(block, sides, width):
    for axis, dim in sides:
        count = lax.axis_size(axis)
        forward = [(i, i + 1) for i in range(count - 1)]
        forward.append((count - 1, 0))
        backward = [(target, source) for source, target in forward]
        low = lax.ppermute(
            lax.slice_in_dim(block, block.shape[dim] - width, None, axis=dim), axis, forward
        )
        high = lax.ppermute(lax.slice_in_dim(block, 0, width, axis=dim), axis, backward)
        block = jnp.concatenate([low, block, high], axis=dim)
    return block


def pair_terms(own_coords, own_alive, far_coords, shift_x, shift_y, same_cell):
    delta_x = shift_x + far_coords[:, 0, None, :] - own_coords[:, 0, :, None]
    delta_y = shift_y + far_coords[:, 1, None, :] - own_coords[:, 1, :, None]
    dist2 = delta_x * delta_x + delta_y * delta_y
    within = jnp.logical_and(dist2 < CUT2, own_alive[:, :, None] > 0.5)
    if same_cell:
        within = jnp.logical_and(within, jnp.logical_not(jnp.eye(dist2.shape[-1], dtype=bool)))
    weight = within.astype(jnp.float32)
    safe = jnp.where(within, dist2, CUT2)
    inverse = 1.0 / safe
    inv_three = inverse * inverse * inverse
    inv_six = inv_three * inv_three
    energy = 4.0 * (inv_six - inv_three) + 1.0
    energy_1 = 4.0 * (3.0 * inv_three - 6.0 * inv_six) * inverse
    energy_2 = 4.0 * (42.0 * inv_six - 12.0 * inv_three) * inverse * inverse
    taper = 1.0 - safe / CUT2
    switch = taper * taper
    switch_1 = -2.0 * taper / CUT2
    switch_2 = 2.0 / (CUT2 * CUT2)
    grad_1 = (energy_1 * switch + energy * switch_1) * weight
    grad_2 = (energy_2 * switch + 2.0 * energy_1 * switch_1 + energy * switch_2) * weight
    pull_x = 2.0 * grad_1 * delta_x
    pull_y = 2.0 * grad_1 * delta_y
    k_xx = (2.0 * grad_1 + 4.0 * grad_2 * delta_x * delta_x).astype(jnp.bfloat16)
    k_xy = (4.0 * grad_2 * delta_x * delta_y).astype(jnp.bfloat16)
    k_yy = (2.0 * grad_1 + 4.0 * grad_2 * delta_y * delta_y).astype(jnp.bfloat16)
    return (pull_x, pull_y, k_xx, k_xy, k_yy)


def apply_rows(k_xx, k_xy, k_yy, far_low):
    gain_x = jnp.einsum(
        "cij,cjv->civ", k_xx, far_low[:, 0], preferred_element_type=jnp.float32
    ) + jnp.einsum("cij,cjv->civ", k_xy, far_low[:, 1], preferred_element_type=jnp.float32)
    gain_y = jnp.einsum(
        "cij,cjv->civ", k_xy, far_low[:, 0], preferred_element_type=jnp.float32
    ) + jnp.einsum("cij,cjv->civ", k_yy, far_low[:, 1], preferred_element_type=jnp.float32)
    return (gain_x, gain_y)


def add_pair(totals, parked, occupied, far_coords, far_low, shift_x, shift_y, same_cell):
    forces_x, forces_y, push_x, push_y, diag_xx, diag_xy, diag_yy = totals
    pull_x, pull_y, k_xx, k_xy, k_yy = pair_terms(
        parked, occupied, far_coords, shift_x, shift_y, same_cell
    )
    gain_x, gain_y = apply_rows(k_xx, k_xy, k_yy, far_low)
    totals = (
        forces_x + jnp.sum(pull_x, axis=2),
        forces_y + jnp.sum(pull_y, axis=2),
        push_x + gain_x,
        push_y + gain_y,
        diag_xx + jnp.sum(k_xx.astype(jnp.float32), axis=2),
        diag_xy + jnp.sum(k_xy.astype(jnp.float32), axis=2),
        diag_yy + jnp.sum(k_yy.astype(jnp.float32), axis=2),
    )
    return (totals, (pull_x, pull_y, k_xx, k_xy, k_yy))


def evaluate(coords, occupied, small_q):
    cell_total = coords.shape[0]
    low = small_q.astype(jnp.bfloat16)
    parked = jnp.concatenate(
        [coords[:, 0:1] + PARK * (1.0 - occupied)[:, None, :], coords[:, 1:2]], axis=1
    )
    empty_rows = jnp.zeros(occupied.shape, jnp.float32)
    empty_push = jnp.zeros(small_q[:, 0].shape, jnp.float32)
    totals = (empty_rows, empty_rows, empty_push, empty_push, empty_rows, empty_rows, empty_rows)
    far_low = padded(low, (("space", 0),), cell_total)
    far_coords = padded(parked, (("space", 0),), cell_total)
    for side in (-1, 0, 1):
        if side == 0:
            block_low = low
            block_coords = parked
        else:
            begin = (1 + side) * cell_total
            block_low = far_low[begin : begin + cell_total]
            block_coords = far_coords[begin : begin + cell_total]
        for lane in (-1, 0, 1):
            totals, unused = add_pair(
                totals,
                parked,
                occupied,
                jnp.roll(block_coords, -lane, axis=0),
                jnp.roll(block_low, -lane, axis=0),
                8.0 * side,
                16.0 * lane,
                side == 0 and lane == 0,
            )
    forces_x, forces_y, push_x, push_y, diag_xx, diag_xy, diag_yy = totals
    wide_own = low.astype(jnp.float32)
    push_x = push_x - diag_xx[..., None] * wide_own[:, 0] - diag_xy[..., None] * wide_own[:, 1]
    push_y = push_y - diag_xy[..., None] * wide_own[:, 0] - diag_yy[..., None] * wide_own[:, 1]
    forces = jnp.stack([forces_x, forces_y], axis=1)
    pushes = jnp.stack([push_x, push_y], axis=1)
    return (forces, pushes)


BLOCK = 128
TILE = 8
BF16 = jnp.bfloat16
F32 = jnp.float32


def matmul(a, b, dims):
    return lax.dot_general(a, b, (dims, ((), ())), preferred_element_type=F32)


def two_parts(a):
    high = a.astype(BF16)
    return high, (a - high.astype(F32)).astype(BF16)


def three_pass(a, b, dims):
    a_high, a_low = two_parts(a)
    b_high, b_low = two_parts(b)
    return matmul(a_high, b_high, dims) + (matmul(a_high, b_low, dims) + matmul(a_low, b_high, dims))


def spread(row, sublane):
    return jnp.broadcast_to(row[sublane : sublane + 1, :], row.shape)


def factor_block(tiles):
    shape = tiles[0].shape
    sub = lax.broadcasted_iota(jnp.int32, shape, 0)
    lane = lax.broadcasted_iota(jnp.int32, shape, 1)
    tiles, rows_out, pivots = list(tiles), [], []
    for j, tile in enumerate(tiles):
        first = TILE * j
        cols = [jnp.broadcast_to(tile[:, first + k : first + k + 1], shape) for k in range(TILE)]
        inverse, ratio, rows = [], {}, []
        pivot = jnp.zeros(shape, F32)
        for k in range(TILE):
            top = spread(cols[k], k)
            pivot = jnp.where(sub == k, top, pivot)
            inverse.append(1.0 / top)
            for m in range(k + 1, TILE):
                ratio[k, m] = spread(cols[m], k) * inverse[k]
                cols[m] = cols[m] - cols[k] * ratio[k, m]
            rows.append(spread(tile, k) + jnp.where(lane == first + k, 1.0, 0.0))
            tile = tile - jnp.where(sub > k, cols[k] * inverse[k], 0.0) * rows[k]
        for i in range(j + 1, len(tiles)):
            cols = [jnp.broadcast_to(tiles[i][:, first + k : first + k + 1], shape) for k in range(TILE)]
            below = tiles[i]
            for k in range(TILE):
                for m in range(k + 1, TILE):
                    cols[m] = cols[m] - cols[k] * ratio[k, m]
                below = below - (cols[k] * inverse[k]) * rows[k]
            tiles[i] = below
        unit = jnp.where(lane < sub + first, tile, jnp.where(lane == sub + first, 1.0, 0.0))
        rows_out.append(unit * lax.rsqrt(pivot))
        pivots.append(pivot)
    return rows_out, pivots


def eliminate(total, work, pivots, small):
    def one_block(step, carry):
        top = pl.multiple_of(step * BLOCK, BLOCK)
        own = pl.ds(top, BLOCK)
        tiles = [work[pl.ds(top + TILE * i, TILE), own] for i in range(BLOCK // TILE)]
        rows_out, pivot_tiles = factor_block(tiles)
        for i in range(BLOCK // TILE):
            pivots[pl.ds(top + TILE * i, TILE), :] = pivot_tiles[i]
            small[TILE * i : TILE * (i + 1), :] = rows_out[i]
        inverse = small[...]

        def scale(col, carry):
            cols = pl.ds(pl.multiple_of(col * BLOCK, BLOCK), BLOCK)
            work[own, cols] = three_pass(inverse, work[own, cols], ((1,), (0,)))
            return carry

        lax.fori_loop(0, total, scale, 0)
        work[own, own] = inverse

        def trail(row, carry):
            rows = pl.ds(pl.multiple_of(row * BLOCK, BLOCK), BLOCK)
            work[rows, own] = jnp.zeros((BLOCK, BLOCK), F32)
            work[rows, :] = work[rows, :] - three_pass(work[own, rows].T, work[own, :], ((1,), (0,)))
            return carry

        lax.fori_loop(step + 1, total, trail, 0)
        return carry

    lax.fori_loop(0, total, one_block, 0)


def gram_kernel(shards, pieces, bc, x_refs, out_refs, part):
    me = lax.axis_index("tangent")
    here = lax.axis_index("space")
    half = bc // 2
    own = x_refs[0][...]
    part[0:bc, :] = matmul(own, own, ((0,), (0,)))
    for k in range(1, shards):
        rows = slice(bc + (k - 1) * half, bc + k * half)
        lower = me < (me ^ k)

        @pl.when(lower)
        def _():
            part[rows, :] = matmul(x_refs[0][:, 0:half], x_refs[k][...], ((0,), (0,)))

        @pl.when(jnp.logical_not(lower))
        def _():
            part[rows, :] = matmul(x_refs[k][:, half:bc], x_refs[0][...], ((0,), (0,)))

    size = part.shape[0] // pieces
    for k in range(pieces):
        start = pl.multiple_of(lax.rem(here + k, pieces) * size, 16)
        out_refs[k][...] = part[pl.ds(start, size), :]


def sum_kernel(in_refs, out_ref):
    total = in_refs[0][...]
    for ref in in_refs[1:]:
        total = total + ref[...]
    out_ref[...] = total


def solve_kernel(shards, pieces, bc, scale, g_refs, x_refs, out_ref, log_ref, work, pivots, small, part):
    me = lax.axis_index("tangent")
    here = lax.axis_index("space")
    half = bc // 2
    size = part.shape[0] // pieces
    for k in range(shards):
        peer = me ^ k
        for j in range(pieces):
            start = pl.multiple_of(lax.rem(here + pieces - j, pieces) * size, 16)
            part[pl.ds(start, size), :] = g_refs[k][j] * scale
        cols = pl.ds(pl.multiple_of(peer * bc, BLOCK), bc)
        work[cols, cols] = part[0:bc, :]
        for j in range(1, shards):
            other = peer ^ j
            low, high = jnp.minimum(peer, other), jnp.maximum(peer, other)
            top = pl.multiple_of(low * bc + jnp.where(peer == high, half, 0), half)
            work[pl.ds(top, half), pl.ds(pl.multiple_of(high * bc, BLOCK), bc)] = part[
                bc + (j - 1) * half : bc + j * half, :
            ]
    eliminate(shards * bc // BLOCK, work, pivots, small)
    mine = pl.ds(pl.multiple_of(me * bc, BLOCK), bc)
    row_block = lax.broadcasted_iota(jnp.int32, (bc, bc), 0) // BLOCK
    col_block = lax.broadcasted_iota(jnp.int32, (bc, bc), 1) // BLOCK

    def times(x_ref, factor):
        high, low = two_parts(factor)
        return matmul(x_ref[...], high, ((1,), (1,))) + matmul(x_ref[...], low, ((1,), (1,)))

    out_ref[...] = times(x_refs[0], jnp.where(row_block >= col_block, work[mine, mine], 0.0))
    for k in range(1, shards):
        peer = me ^ k

        @pl.when(peer < me)
        def _():
            cols = pl.ds(pl.multiple_of(peer * bc, BLOCK), bc)
            out_ref[...] += times(x_refs[k], work[mine, cols])

    eye = lax.broadcasted_iota(jnp.int32, (BLOCK, BLOCK), 0) == lax.broadcasted_iota(jnp.int32, (BLOCK, BLOCK), 1)
    for a in range(bc // BLOCK):
        block = pivots[pl.ds(pl.multiple_of(me * bc + a * BLOCK, BLOCK), BLOCK), :]
        log_ref[:, a * BLOCK : (a + 1) * BLOCK] = 0.5 * jnp.log(
            jnp.sum(jnp.where(eye, block, 0.0), axis=0, keepdims=True)
        )


def call(kernel, counts, out_shapes, scratch, operands):
    def unpacked(*refs):
        groups, at = [], 0
        for count in counts:
            groups.append(refs[at : at + count])
            at += count
        kernel(*groups, *refs[at:])

    return pl.pallas_call(
        unpacked,
        out_shape=out_shapes,
        scratch_shapes=scratch,
        compiler_params=pltpu.CompilerParams(vmem_limit_bytes=48 * 1024 * 1024),
    )(*operands)


def flip(array, axis, bit):
    return lax.ppermute(array, axis, [(i, i ^ bit) for i in range(lax.axis_size(axis))])


def orthonormalize(x):
    shards, pieces = lax.axis_size("tangent"), lax.axis_size("space")
    rows, bc = x.shape
    blocks = {0: x}
    bit = shards // 2
    while bit:
        blocks.update({k ^ bit: flip(v, "tangent", bit) for k, v in list(blocks.items())})
        bit //= 2
    blocks = [blocks[k] for k in range(shards)]
    held = bc + (shards - 1) * (bc // 2)
    direct = pieces <= 8
    cuts = pieces if direct else 1
    size = held // cuts
    piece = jax.ShapeDtypeStruct((size, bc), F32)

    def gram(*refs):
        gram_kernel(shards, cuts, bc, *refs)

    parts = call(
        gram, (shards, cuts), (piece,) * cuts, [pltpu.VMEM((held, bc), F32)], blocks
    )
    if direct:
        arrived = [parts[0]]
        for k in range(1, pieces):
            arrived.append(lax.ppermute(parts[k], "space", [(i, (i + k) % pieces) for i in range(pieces)]))
        total = call(lambda a, out: sum_kernel(a, out), (pieces,), piece, [], arrived)
        around = [total]
        for k in range(1, pieces):
            around.append(lax.ppermute(total, "space", [(i, (i + k) % pieces) for i in range(pieces)]))
        total = jnp.stack(around)
    else:
        total = lax.psum(parts[0], "space")[None]
    totals = {0: total}
    bit = shards // 2
    while bit:
        totals.update({k ^ bit: flip(v, "tangent", bit) for k, v in list(totals.items())})
        bit //= 2
    totals = [totals[k] for k in range(shards)]
    scale = 1.0 / (float(rows) * pieces)

    def solve(g_refs, x_refs, *refs):
        solve_kernel(shards, cuts, bc, scale, g_refs, x_refs, *refs)

    full = shards * bc
    out, logs = call(
        solve,
        (shards, shards),
        (jax.ShapeDtypeStruct((rows, bc), F32), jax.ShapeDtypeStruct((1, bc), F32)),
        [
            pltpu.VMEM((full, full), F32),
            pltpu.VMEM((full, BLOCK), F32),
            pltpu.VMEM((BLOCK, BLOCK), F32),
            pltpu.VMEM((held, bc), F32),
        ],
        totals + blocks,
    )
    return out, logs[0]


def body(positions, momenta, cell_count, tangent):
    cell_total = positions.shape[0]
    slot_count = positions.shape[2]
    occupied = (
        lax.broadcasted_iota(jnp.int32, (cell_total, slot_count), 1) < cell_count[:, None]
    ).astype(jnp.float32)
    state = tangent * occupied[:, None, :, None]
    coords = positions
    speeds = momenta
    small_q = state[:, 0:2]
    small_p = state[:, 2:4]
    forces, pushes = evaluate(coords, occupied, small_q)
    for step_index in range(STEPS):
        midway_p = speeds + 0.5 * DT * forces
        midway_dp = small_p + 0.5 * DT * pushes
        coords = coords + DT * midway_p
        small_q = small_q + DT * midway_dp
        forces, pushes = evaluate(coords, occupied, small_q)
        speeds = midway_p + 0.5 * DT * forces
        small_p = midway_dp + 0.5 * DT * pushes
    phase = jnp.concatenate([coords, speeds], axis=1)
    final = jnp.concatenate([small_q, small_p], axis=1)
    shape = final.shape
    out, stretch = orthonormalize(final.astype(BF16).reshape(-1, shape[3]))
    return (phase, out.reshape(shape), stretch)


def solution(mesh):
    placed = (
        P(("groups", "space"), None, None),
        P(("groups", "space"), None, None),
        P(("groups", "space")),
        P(("groups", "space"), None, None, "tangent"),
    )
    return jax.shard_map(
        body,
        mesh=mesh,
        in_specs=placed,
        out_specs=(
            P(("groups", "space"), None, None),
            P(("groups", "space"), None, None, "tangent"),
            P(("groups", "tangent")),
        ),
        check_vma=False,
    )
```

```python
import jax
import jax.numpy as jnp
from jax import lax
from jax.experimental import pallas as pl
from jax.experimental.pallas import tpu as pltpu
from jax.sharding import PartitionSpec as P

STEPS = 2


DT = 0.005
CUT2 = 2.0 ** (1.0 / 3.0)
WIDE, TALL = 8, 16


BLOCK = 128
TILE = 8
BF16 = jnp.bfloat16
F32 = jnp.float32


def matmul(a, b, dims):
    return lax.dot_general(a, b, (dims, ((), ())), preferred_element_type=F32)


def two_parts(a):
    high = a.astype(BF16)
    return high, (a - high.astype(F32)).astype(BF16)


def three_pass(a, b, dims):
    a_high, a_low = two_parts(a)
    b_high, b_low = two_parts(b)
    return matmul(a_high, b_high, dims) + (matmul(a_high, b_low, dims) + matmul(a_low, b_high, dims))


def spread(row, sublane):
    return jnp.broadcast_to(row[sublane : sublane + 1, :], row.shape)


def factor_block(tiles):
    shape = tiles[0].shape
    sub = lax.broadcasted_iota(jnp.int32, shape, 0)
    lane = lax.broadcasted_iota(jnp.int32, shape, 1)
    tiles, rows_out, pivots = list(tiles), [], []
    for j, tile in enumerate(tiles):
        first = TILE * j
        cols = [jnp.broadcast_to(tile[:, first + k : first + k + 1], shape) for k in range(TILE)]
        inverse, ratio, rows = [], {}, []
        pivot = jnp.zeros(shape, F32)
        for k in range(TILE):
            top = spread(cols[k], k)
            pivot = jnp.where(sub == k, top, pivot)
            inverse.append(1.0 / top)
            for m in range(k + 1, TILE):
                ratio[k, m] = spread(cols[m], k) * inverse[k]
                cols[m] = cols[m] - cols[k] * ratio[k, m]
            rows.append(spread(tile, k) + jnp.where(lane == first + k, 1.0, 0.0))
            tile = tile - jnp.where(sub > k, cols[k] * inverse[k], 0.0) * rows[k]
        for i in range(j + 1, len(tiles)):
            cols = [jnp.broadcast_to(tiles[i][:, first + k : first + k + 1], shape) for k in range(TILE)]
            below = tiles[i]
            for k in range(TILE):
                for m in range(k + 1, TILE):
                    cols[m] = cols[m] - cols[k] * ratio[k, m]
                below = below - (cols[k] * inverse[k]) * rows[k]
            tiles[i] = below
        unit = jnp.where(lane < sub + first, tile, jnp.where(lane == sub + first, 1.0, 0.0))
        rows_out.append(unit * lax.rsqrt(pivot))
        pivots.append(pivot)
    return rows_out, pivots


def eliminate(total, work, pivots, small):
    def one_block(step, carry):
        top = pl.multiple_of(step * BLOCK, BLOCK)
        own = pl.ds(top, BLOCK)
        tiles = [work[pl.ds(top + TILE * i, TILE), own] for i in range(BLOCK // TILE)]
        rows_out, pivot_tiles = factor_block(tiles)
        for i in range(BLOCK // TILE):
            pivots[pl.ds(top + TILE * i, TILE), :] = pivot_tiles[i]
            small[TILE * i : TILE * (i + 1), :] = rows_out[i]
        inverse = small[...]

        def scale(col, carry):
            cols = pl.ds(pl.multiple_of(col * BLOCK, BLOCK), BLOCK)
            work[own, cols] = three_pass(inverse, work[own, cols], ((1,), (0,)))
            return carry

        lax.fori_loop(0, total, scale, 0)
        work[own, own] = inverse

        def trail(row, carry):
            rows = pl.ds(pl.multiple_of(row * BLOCK, BLOCK), BLOCK)
            work[rows, own] = jnp.zeros((BLOCK, BLOCK), F32)
            work[rows, :] = work[rows, :] - three_pass(work[own, rows].T, work[own, :], ((1,), (0,)))
            return carry

        lax.fori_loop(step + 1, total, trail, 0)
        return carry

    lax.fori_loop(0, total, one_block, 0)


def gram_kernel(shards, pieces, bc, x_refs, out_refs, part):
    me = lax.axis_index("tangent")
    here = lax.axis_index("space")
    half = bc // 2
    own = x_refs[0][...]
    part[0:bc, :] = matmul(own, own, ((0,), (0,)))
    for k in range(1, shards):
        rows = slice(bc + (k - 1) * half, bc + k * half)
        lower = me < (me ^ k)

        @pl.when(lower)
        def _():
            part[rows, :] = matmul(x_refs[0][:, 0:half], x_refs[k][...], ((0,), (0,)))

        @pl.when(jnp.logical_not(lower))
        def _():
            part[rows, :] = matmul(x_refs[k][:, half:bc], x_refs[0][...], ((0,), (0,)))

    size = part.shape[0] // pieces
    for k in range(pieces):
        start = pl.multiple_of(lax.rem(here + k, pieces) * size, 16)
        out_refs[k][...] = part[pl.ds(start, size), :]


def sum_kernel(in_refs, out_ref):
    total = in_refs[0][...]
    for ref in in_refs[1:]:
        total = total + ref[...]
    out_ref[...] = total


def solve_kernel(shards, pieces, bc, scale, g_refs, x_refs, out_ref, log_ref, work, pivots, small, part):
    me = lax.axis_index("tangent")
    here = lax.axis_index("space")
    half = bc // 2
    size = part.shape[0] // pieces
    for k in range(shards):
        peer = me ^ k
        for j in range(pieces):
            start = pl.multiple_of(lax.rem(here + pieces - j, pieces) * size, 16)
            part[pl.ds(start, size), :] = g_refs[k][j] * scale
        cols = pl.ds(pl.multiple_of(peer * bc, BLOCK), bc)
        work[cols, cols] = part[0:bc, :]
        for j in range(1, shards):
            other = peer ^ j
            low, high = jnp.minimum(peer, other), jnp.maximum(peer, other)
            top = pl.multiple_of(low * bc + jnp.where(peer == high, half, 0), half)
            work[pl.ds(top, half), pl.ds(pl.multiple_of(high * bc, BLOCK), bc)] = part[
                bc + (j - 1) * half : bc + j * half, :
            ]
    eliminate(shards * bc // BLOCK, work, pivots, small)
    mine = pl.ds(pl.multiple_of(me * bc, BLOCK), bc)
    row_block = lax.broadcasted_iota(jnp.int32, (bc, bc), 0) // BLOCK
    col_block = lax.broadcasted_iota(jnp.int32, (bc, bc), 1) // BLOCK

    def times(x_ref, factor):
        high, low = two_parts(factor)
        return matmul(x_ref[...], high, ((1,), (1,))) + matmul(x_ref[...], low, ((1,), (1,)))

    out_ref[...] = times(x_refs[0], jnp.where(row_block >= col_block, work[mine, mine], 0.0))
    for k in range(1, shards):
        peer = me ^ k

        @pl.when(peer < me)
        def _():
            cols = pl.ds(pl.multiple_of(peer * bc, BLOCK), bc)
            out_ref[...] += times(x_refs[k], work[mine, cols])

    eye = lax.broadcasted_iota(jnp.int32, (BLOCK, BLOCK), 0) == lax.broadcasted_iota(jnp.int32, (BLOCK, BLOCK), 1)
    for a in range(bc // BLOCK):
        block = pivots[pl.ds(pl.multiple_of(me * bc + a * BLOCK, BLOCK), BLOCK), :]
        log_ref[:, a * BLOCK : (a + 1) * BLOCK] = 0.5 * jnp.log(
            jnp.sum(jnp.where(eye, block, 0.0), axis=0, keepdims=True)
        )


def call(kernel, counts, out_shapes, scratch, operands):
    def unpacked(*refs):
        groups, at = [], 0
        for count in counts:
            groups.append(refs[at : at + count])
            at += count
        kernel(*groups, *refs[at:])

    return pl.pallas_call(
        unpacked,
        out_shape=out_shapes,
        scratch_shapes=scratch,
        compiler_params=pltpu.CompilerParams(vmem_limit_bytes=48 * 1024 * 1024),
    )(*operands)


def flip(array, axis, bit):
    return lax.ppermute(array, axis, [(i, i ^ bit) for i in range(lax.axis_size(axis))])


def orthonormalize(x):
    shards, pieces = lax.axis_size("tangent"), lax.axis_size("space")
    rows, bc = x.shape
    blocks = {0: x}
    bit = shards // 2
    while bit:
        blocks.update({k ^ bit: flip(v, "tangent", bit) for k, v in list(blocks.items())})
        bit //= 2
    blocks = [blocks[k] for k in range(shards)]
    held = bc + (shards - 1) * (bc // 2)
    direct = pieces <= 8
    cuts = pieces if direct else 1
    size = held // cuts
    piece = jax.ShapeDtypeStruct((size, bc), F32)

    def gram(*refs):
        gram_kernel(shards, cuts, bc, *refs)

    parts = call(
        gram, (shards, cuts), (piece,) * cuts, [pltpu.VMEM((held, bc), F32)], blocks
    )
    if direct:
        arrived = [parts[0]]
        for k in range(1, pieces):
            arrived.append(lax.ppermute(parts[k], "space", [(i, (i + k) % pieces) for i in range(pieces)]))
        total = call(lambda a, out: sum_kernel(a, out), (pieces,), piece, [], arrived)
        around = [total]
        for k in range(1, pieces):
            around.append(lax.ppermute(total, "space", [(i, (i + k) % pieces) for i in range(pieces)]))
        total = jnp.stack(around)
    else:
        total = lax.psum(parts[0], "space")[None]
    totals = {0: total}
    bit = shards // 2
    while bit:
        totals.update({k ^ bit: flip(v, "tangent", bit) for k, v in list(totals.items())})
        bit //= 2
    totals = [totals[k] for k in range(shards)]
    scale = 1.0 / (float(rows) * pieces)

    def solve(g_refs, x_refs, *refs):
        solve_kernel(shards, cuts, bc, scale, g_refs, x_refs, *refs)

    full = shards * bc
    out, logs = call(
        solve,
        (shards, shards),
        (jax.ShapeDtypeStruct((rows, bc), F32), jax.ShapeDtypeStruct((1, bc), F32)),
        [
            pltpu.VMEM((full, full), F32),
            pltpu.VMEM((full, BLOCK), F32),
            pltpu.VMEM((BLOCK, BLOCK), F32),
            pltpu.VMEM((held, bc), F32),
        ],
        totals + blocks,
    )
    return out, logs[0]


def lattice_rows(raw_ref, first, count):
    cells = raw_ref.shape[0]
    high = cells * TALL
    sites = [
        raw_ref[c, 0:1, :].astype(jnp.int32) * high + raw_ref[c, 1:2, :].astype(jnp.int32) + c * TALL
        for c in range(cells)
    ]
    site = jnp.concatenate(sites, axis=1)
    rows = lax.broadcasted_iota(jnp.int32, (count, site.shape[1]), 0) + first
    return jnp.where(rows == site, 1.0, 0.0).astype(BF16)


def three_parts(a):
    high, rest = a.astype(BF16), None
    rest = a - high.astype(F32)
    mid = rest.astype(BF16)
    return high, mid, (rest - mid.astype(F32)).astype(BF16)


def sort_kernel(raw_ref, count_ref, tangent_ref, state_ref, left_ref, right_ref):
    cells, comps, slots, bc = tangent_ref.shape
    high = cells * TALL
    place = lattice_rows(raw_ref, 0, high * WIDE)
    slot = lax.broadcasted_iota(jnp.int32, (slots, bc), 0)
    for comp in range(comps):
        rows = [jnp.where(slot < count_ref[c], tangent_ref[c, comp], 0.0) for c in range(cells)]
        top, low = two_parts(jnp.concatenate(rows, axis=0))
        moved = matmul(place, top, ((1,), (0,))) + matmul(place, low, ((1,), (0,)))
        state_ref[comp] = moved.reshape(WIDE, high, bc)
        near = moved.astype(BF16).reshape(WIDE, high, bc)
        if comp < 2:
            left_ref[3 * comp : 3 * comp + 3] = near[0:3]
            right_ref[3 * comp : 3 * comp + 3] = near[WIDE - 3 :]
        else:
            at = 6 + 2 * (comp - 2)
            left_ref[at : at + 2] = near[0:2]
            right_ref[at : at + 2] = near[WIDE - 2 :]


def bond(far_x, far_y, own_x, own_y, both, shift_x, shift_y):
    dx = shift_x + far_x - own_x
    dy = shift_y + far_y - own_y
    dist2 = dx * dx + dy * dy
    within = jnp.logical_and(dist2 < CUT2, both > 0.5)
    weight = jnp.where(within, 1.0, 0.0)
    safe = jnp.where(within, dist2, CUT2)
    inverse = 1.0 / safe
    inv_three = inverse * inverse * inverse
    inv_six = inv_three * inv_three
    energy = 4.0 * (inv_six - inv_three) + 1.0
    energy_1 = 4.0 * (3.0 * inv_three - 6.0 * inv_six) * inverse
    energy_2 = 4.0 * (42.0 * inv_six - 12.0 * inv_three) * inverse * inverse
    taper = 1.0 - safe * (1.0 / CUT2)
    switch = taper * taper
    switch_1 = taper * (-2.0 / CUT2)
    switch_2 = 2.0 / (CUT2 * CUT2)
    twice_1 = (energy_1 * switch + energy * switch_1) * weight * 2.0
    four_2 = (energy_2 * switch + 2.0 * energy_1 * switch_1 + energy * switch_2) * weight * 4.0
    k_xx = twice_1 + four_2 * dx * dx
    k_xy = four_2 * dx * dy
    k_yy = twice_1 + four_2 * dy * dy
    return twice_1 * dx, twice_1 * dy, (k_xx, k_xy, k_yy)


def up(a):
    return pltpu.roll(a, a.shape[0] - 1, 0)


def down(a):
    return pltpu.roll(a, 1, 0)


KICKS = tuple((0.5 if step in (0, STEPS) else 1.0) * DT for step in range(STEPS + 1))


def path_kernel(raw_ref, low_ref, high_ref, phase_ref, k_ref, lat):
    cells, _, slots = raw_ref.shape
    tall = cells * TALL
    halo = STEPS + 1
    columns = WIDE + 2 * halo
    own = lattice_rows(raw_ref, 0, WIDE * tall)
    sides = (
        (low_ref, lattice_rows(low_ref, (WIDE - halo) * tall, halo * tall), 0, halo),
        (raw_ref, own, halo, WIDE),
        (high_ref, lattice_rows(high_ref, 0, halo * tall), halo + WIDE, halo),
    )
    for ref, place, first, width in sides:
        for item in range(5):
            row = jnp.concatenate([ref[c, item : item + 1, :] for c in range(cells)], axis=1)
            wide = jnp.broadcast_to(row, (BLOCK, row.shape[1]))
            parts = three_parts(wide) if item < 4 else (wide.astype(BF16),)
            value = sum(matmul(place, part, ((1,), (1,))) for part in parts)
            lat[item, first : first + width] = value.reshape(width, tall, BLOCK)
    site = lax.broadcasted_iota(jnp.int32, (tall, BLOCK), 0)
    shift_y = jnp.where(lax.rem(site, TALL) == TALL - 1, float(TALL), 0.0)
    zero = jnp.zeros((tall, BLOCK), F32)
    for step, kick in enumerate(KICKS):
        move = DT if step < STEPS else 0.0

        def column(c, carry):
            x, y, alive, pull_x, pull_y = carry
            far_x, far_y, far_alive = lat[0, c + 1], lat[1, c + 1], lat[4, c + 1]
            crossing = jnp.logical_or(c == halo - 1, c == halo + WIDE - 1)
            shift_x = jnp.where(crossing, float(WIDE), 0.0)
            side_x, side_y, k_side = bond(far_x, far_y, x, y, alive * far_alive, shift_x, 0.0)
            over_x, over_y, k_over = bond(up(x), up(y), x, y, alive * up(alive), 0.0, shift_y)
            for a in range(3):
                k_ref[step, a, c] = k_side[a].astype(BF16)
                k_ref[step, 3 + a, c] = k_over[a].astype(BF16)
            speed_x = lat[2, c] + kick * (side_x - pull_x + over_x - down(over_x))
            speed_y = lat[3, c] + kick * (side_y - pull_y + over_y - down(over_y))
            lat[2, c], lat[3, c] = speed_x, speed_y
            if move:
                lat[0, c], lat[1, c] = x + move * speed_x, y + move * speed_y
            return far_x, far_y, far_alive, side_x, side_y

        start = (lat[0, step], lat[1, step], lat[4, step], zero, zero)
        lax.fori_loop(step, columns - 1 - step, column, start)
    for item in range(4):
        value = lat[item, halo : halo + WIDE, :, 0:TILE].reshape(WIDE * tall, TILE)
        back = sum(matmul(part, own, ((0,), (0,))) for part in three_parts(value))
        for c in range(cells):
            phase_ref[c, item : item + 1, :] = back[0:1, c * slots : (c + 1) * slots]


def tangent_kernel(raw_ref, k_ref, state_ref, low_ref, high_ref, x_ref, wide):
    cells, comps, slots, bc = x_ref.shape
    tall = cells * TALL
    halo = STEPS + 1
    columns = WIDE + 2 * halo
    for comp in range(comps):
        wide[comp, halo : halo + WIDE] = state_ref[comp]
        if comp < 2:
            wide[comp, 0:halo] = low_ref[3 * comp : 3 * comp + 3].astype(F32)
            wide[comp, halo + WIDE :] = high_ref[3 * comp : 3 * comp + 3].astype(F32)
        else:
            at = 6 + 2 * (comp - 2)
            wide[comp, 1:halo] = low_ref[at : at + 2].astype(F32)
            wide[comp, halo + WIDE : columns - 1] = high_ref[at : at + 2].astype(F32)
    zero = jnp.zeros((tall, bc), F32)

    def rounded(comp, c):
        return wide[comp, c].astype(BF16).astype(F32)

    def stretched(step, a, c):
        k = k_ref[step, a, c].astype(F32)
        return jnp.concatenate([k] * (bc // BLOCK), axis=1)

    for step, kick in enumerate(KICKS):
        move = DT if step < STEPS else 0.0

        def push(c, k0, e_x, e_y):
            k_xx, k_xy, k_yy = [stretched(step, k0 + a, c) for a in range(3)]
            return k_xx * e_x + k_xy * e_y, k_xy * e_x + k_yy * e_y

        def column(c, carry):
            x, y, pull_x, pull_y = carry
            far_x, far_y = rounded(0, c + 1), rounded(1, c + 1)
            side_x, side_y = push(c, 0, far_x - x, far_y - y)
            over_x, over_y = push(c, 3, up(x) - x, up(y) - y)
            speed_x = wide[2, c] + kick * (side_x - pull_x + over_x - down(over_x))
            speed_y = wide[3, c] + kick * (side_y - pull_y + over_y - down(over_y))
            wide[2, c], wide[3, c] = speed_x, speed_y
            if move:
                wide[0, c] = wide[0, c] + move * speed_x
                wide[1, c] = wide[1, c] + move * speed_y
            return far_x, far_y, side_x, side_y

        x, y = rounded(0, step), rounded(1, step)
        first = push(step, 0, rounded(0, step + 1) - x, rounded(1, step + 1) - y)
        start = (rounded(0, step + 1), rounded(1, step + 1)) + first
        lax.fori_loop(step + 1, columns - 1 - step, column, start)
    place = lattice_rows(raw_ref, 0, WIDE * tall)
    for comp in range(comps):
        value = wide[comp, halo : halo + WIDE].reshape(WIDE * tall, bc).astype(BF16)
        back = matmul(place, value, ((0,), (0,))).astype(BF16)
        for c in range(cells):
            x_ref[c, comp] = back[c * slots : (c + 1) * slots]


def dynamics(positions, momenta, cell_count, tangent):
    cells, comps, slots, bc = tangent.shape
    tall = cells * TALL
    columns = WIDE + 2 * (STEPS + 1)
    occupied = (lax.broadcasted_iota(jnp.int32, (cells, 1, slots), 2) < cell_count[:, None, None]).astype(F32)
    raw = jnp.concatenate([positions, momenta, occupied], axis=1)
    count = lax.axis_size("space")
    forward = [(i, (i + 1) % count) for i in range(count)]
    backward = [(b, a) for a, b in forward]
    raw_low, raw_high = lax.ppermute(raw, "space", forward), lax.ppermute(raw, "space", backward)
    halo = jax.ShapeDtypeStruct((10, tall, bc), BF16)
    vmem = pl.BlockSpec(memory_space=pltpu.VMEM)
    params = pltpu.CompilerParams(vmem_limit_bytes=48 * 1024 * 1024)
    state, left, right = pl.pallas_call(
        sort_kernel,
        out_shape=(jax.ShapeDtypeStruct((comps, WIDE, tall, bc), F32), halo, halo),
        in_specs=[vmem, pl.BlockSpec(memory_space=pltpu.SMEM), vmem],
        compiler_params=params,
    )(raw, cell_count, tangent)
    low, high = lax.ppermute(right, "space", forward), lax.ppermute(left, "space", backward)
    phase, k = pl.pallas_call(
        path_kernel,
        out_shape=(
            jax.ShapeDtypeStruct((cells, 4, slots), F32),
            jax.ShapeDtypeStruct((STEPS + 1, 6, columns, tall, BLOCK), BF16),
        ),
        scratch_shapes=[pltpu.VMEM((5, columns, tall, BLOCK), F32)],
        compiler_params=params,
        cost_estimate=pl.CostEstimate(flops=4 * 10**9, bytes_accessed=4 * 10**6, transcendentals=0),
    )(raw, raw_low, raw_high)
    x = pl.pallas_call(
        tangent_kernel,
        out_shape=jax.ShapeDtypeStruct(tangent.shape, BF16),
        scratch_shapes=[pltpu.VMEM((comps, columns, tall, bc), F32)],
        compiler_params=params,
    )(raw, k, state, low, high)
    return phase, x


def body(positions, momenta, cell_count, tangent):
    phase, x = dynamics(positions, momenta, cell_count, tangent)
    out, stretch = orthonormalize(x.reshape(-1, x.shape[3]))
    return (phase, out.reshape(x.shape), stretch)


def solution(mesh):
    placed = (
        P(("groups", "space"), None, None),
        P(("groups", "space"), None, None),
        P(("groups", "space")),
        P(("groups", "space"), None, None, "tangent"),
    )
    return jax.shard_map(
        body,
        mesh=mesh,
        in_specs=placed,
        out_specs=(
            P(("groups", "space"), None, None),
            P(("groups", "space"), None, None, "tangent"),
            P(("groups", "tangent")),
        ),
        check_vma=False,
    )
```

```python
import jax
import jax.numpy as jnp
from jax import lax
from jax.experimental import pallas as pl
from jax.experimental.pallas import tpu as pltpu
from jax.sharding import PartitionSpec as P

STEPS = 2


DT = 0.005
CUT2 = 2.0 ** (1.0 / 3.0)
WIDE, TALL = 8, 16


BLOCK = 128
TILE = 8
NEAR = 3
BF16 = jnp.bfloat16
F32 = jnp.float32


def matmul(a, b, dims):
    return lax.dot_general(a, b, (dims, ((), ())), preferred_element_type=F32)


def two_parts(a):
    high = a.astype(BF16)
    return high, (a - high.astype(F32)).astype(BF16)


def three_pass(a, b, axis_a):
    a_high, a_low = two_parts(a)
    b_high, b_low = two_parts(b)
    left = jnp.concatenate([a_high, a_high, a_low], axis=axis_a)
    right = jnp.concatenate([b_high, b_low, b_high], axis=0)
    return matmul(left, right, ((axis_a,), (0,)))


def spread(row, sublane):
    return jnp.broadcast_to(row[sublane : sublane + 1, :], row.shape)


def columns_of(tile, group):
    return [jnp.broadcast_to(tile[:, k : k + 1], tile.shape) for k in range(TILE * group, TILE * (group + 1))]


def factor_block(tiles):
    shape = tiles[0].shape
    sub = lax.broadcasted_iota(jnp.int32, shape, 0)
    lane = lax.broadcasted_iota(jnp.int32, shape, 1)
    tiles, rows_out, pivots = list(tiles), [], []
    cols = columns_of(tiles[0], 0)
    for j, tile in enumerate(tiles):
        first, more = TILE * j, j + 1 < len(tiles)
        if more:
            ahead, cols_next, ahead_next = (
                columns_of(tile, j + 1), columns_of(tiles[j + 1], j), columns_of(tiles[j + 1], j + 1)
            )
        inverse, ratio, rows = [], {}, []
        pivot = jnp.zeros(shape, F32)
        for k in range(TILE):
            top = spread(cols[k], k)
            pivot = jnp.where(sub == k, top, pivot)
            inverse.append(1.0 / top)
            for m in range(k + 1, TILE):
                ratio[k, m] = spread(cols[m], k) * inverse[k]
                cols[m] = cols[m] - cols[k] * ratio[k, m]
            rows.append(spread(tile, k) + jnp.where(lane == first + k, 1.0, 0.0))
            tile = tile - jnp.where(sub > k, cols[k] * inverse[k], 0.0) * rows[k]
            if more:
                for m in range(TILE):
                    part = spread(ahead[m], k) * inverse[k]
                    ahead[m] = ahead[m] - cols[k] * part
                    ahead_next[m] = ahead_next[m] - cols_next[k] * part
                for m in range(k + 1, TILE):
                    cols_next[m] = cols_next[m] - cols_next[k] * ratio[k, m]
                tiles[j + 1] = tiles[j + 1] - (cols_next[k] * inverse[k]) * rows[k]
        root = lax.rsqrt(pivot)
        unit = jnp.where(lane < sub + first, tile, jnp.where(lane == sub + first, 1.0, 0.0)) * root
        rows_out.append(unit)
        near = min(j + 1 + NEAR, len(tiles))
        if near < len(tiles):
            scaled = jnp.where(lane < first + TILE, unit, tile * root)
            high, low = [part.astype(F32) for part in two_parts(scaled)]
            left = jnp.concatenate([high, high, low], axis=0)[:, TILE * near :]
            right = jnp.concatenate([high, low, high], axis=0)
            update = matmul(left.astype(BF16), right.astype(BF16), ((0,), (0,)))
            group = jnp.logical_and(lane >= first, lane < first + TILE)
            for i in range(near, len(tiles)):
                at = TILE * (i - near)
                tiles[i] = jnp.where(group, 0.0, tiles[i]) - update[at : at + TILE, :]
        for i in range(j + 2, near):
            low, below = columns_of(tiles[i], j), tiles[i]
            for k in range(TILE):
                for m in range(k + 1, TILE):
                    low[m] = low[m] - low[k] * ratio[k, m]
                below = below - (low[k] * inverse[k]) * rows[k]
            tiles[i] = below
        pivots.append(pivot)
        if more:
            cols = ahead_next
    return rows_out, pivots


def eliminate(total, work, pivots, small):
    def one_block(step, carry):
        top = pl.multiple_of(step * BLOCK, BLOCK)
        own = pl.ds(top, BLOCK)
        tiles = [work[pl.ds(top + TILE * i, TILE), own] for i in range(BLOCK // TILE)]
        rows_out, pivot_tiles = factor_block(tiles)
        for i in range(BLOCK // TILE):
            pivots[pl.ds(top + TILE * i, TILE), :] = pivot_tiles[i]
            small[TILE * i : TILE * (i + 1), :] = rows_out[i]
        inverse = small[...]
        work[own, :] = three_pass(inverse, work[own, :], 1)
        work[own, own] = inverse
        for now in range(total - 1):

            @pl.when(step == now)
            def _():
                here, rest = slice(now * BLOCK, (now + 1) * BLOCK), slice((now + 1) * BLOCK, total * BLOCK)
                work[rest, here] = jnp.zeros(((total - 1 - now) * BLOCK, BLOCK), F32)
                work[rest, :] = work[rest, :] - three_pass(work[here, rest], work[here, :], 0)

        return carry

    lax.fori_loop(0, total, one_block, 0)


def gram_kernel(shards, pieces, bc, x_refs, out_refs, part):
    me = lax.axis_index("tangent")
    here = lax.axis_index("space")
    half = bc // 2
    own = x_refs[0][...]
    part[0:bc, :] = matmul(own, own, ((0,), (0,)))
    for k in range(1, shards):
        rows = slice(bc + (k - 1) * half, bc + k * half)
        lower = me < (me ^ k)

        @pl.when(lower)
        def _():
            part[rows, :] = matmul(x_refs[0][:, 0:half], x_refs[k][...], ((0,), (0,)))

        @pl.when(jnp.logical_not(lower))
        def _():
            part[rows, :] = matmul(x_refs[k][:, half:bc], x_refs[0][...], ((0,), (0,)))

    size = part.shape[0] // pieces
    for k in range(pieces):
        start = pl.multiple_of(lax.rem(here + k, pieces) * size, 16)
        out_refs[k][...] = part[pl.ds(start, size), :]


def sum_kernel(in_refs, out_ref):
    total = in_refs[0][...]
    for ref in in_refs[1:]:
        total = total + ref[...]
    out_ref[...] = total


def solve_kernel(shards, pieces, bc, scale, g_refs, x_refs, out_ref, log_ref, work, pivots, small, part):
    me = lax.axis_index("tangent")
    here = lax.axis_index("space")
    half = bc // 2
    size = part.shape[0] // pieces
    for k in range(shards):
        peer = me ^ k
        for j in range(pieces):
            start = pl.multiple_of(lax.rem(here + pieces - j, pieces) * size, 16)
            part[pl.ds(start, size), :] = g_refs[k][j] * scale
        cols = pl.ds(pl.multiple_of(peer * bc, BLOCK), bc)
        work[cols, cols] = part[0:bc, :]
        for j in range(1, shards):
            other = peer ^ j
            low, high = jnp.minimum(peer, other), jnp.maximum(peer, other)
            top = pl.multiple_of(low * bc + jnp.where(peer == high, half, 0), half)
            work[pl.ds(top, half), pl.ds(pl.multiple_of(high * bc, BLOCK), bc)] = part[
                bc + (j - 1) * half : bc + j * half, :
            ]
    eliminate(shards * bc // BLOCK, work, pivots, small)
    mine = pl.ds(pl.multiple_of(me * bc, BLOCK), bc)
    row_block = lax.broadcasted_iota(jnp.int32, (bc, bc), 0) // BLOCK
    col_block = lax.broadcasted_iota(jnp.int32, (bc, bc), 1) // BLOCK

    def times(x_ref, factor):
        high, low = two_parts(factor)
        return matmul(x_ref[...], high, ((1,), (1,))) + matmul(x_ref[...], low, ((1,), (1,)))

    out_ref[...] = times(x_refs[0], jnp.where(row_block >= col_block, work[mine, mine], 0.0))
    for k in range(1, shards):
        peer = me ^ k

        @pl.when(peer < me)
        def _():
            cols = pl.ds(pl.multiple_of(peer * bc, BLOCK), bc)
            out_ref[...] += times(x_refs[k], work[mine, cols])

    eye = lax.broadcasted_iota(jnp.int32, (BLOCK, BLOCK), 0) == lax.broadcasted_iota(jnp.int32, (BLOCK, BLOCK), 1)
    for a in range(bc // BLOCK):
        block = pivots[pl.ds(pl.multiple_of(me * bc + a * BLOCK, BLOCK), BLOCK), :]
        log_ref[:, a * BLOCK : (a + 1) * BLOCK] = 0.5 * jnp.log(
            jnp.sum(jnp.where(eye, block, 0.0), axis=0, keepdims=True)
        )


def call(kernel, counts, out_shapes, scratch, operands):
    def unpacked(*refs):
        groups, at = [], 0
        for count in counts:
            groups.append(refs[at : at + count])
            at += count
        kernel(*groups, *refs[at:])

    return pl.pallas_call(
        unpacked,
        out_shape=out_shapes,
        scratch_shapes=scratch,
        compiler_params=pltpu.CompilerParams(vmem_limit_bytes=48 * 1024 * 1024),
    )(*operands)


def flip(array, axis, bit):
    return lax.ppermute(array, axis, [(i, i ^ bit) for i in range(lax.axis_size(axis))])


def orthonormalize(x):
    shards, pieces = lax.axis_size("tangent"), lax.axis_size("space")
    rows, bc = x.shape
    blocks = {0: x}
    bit = shards // 2
    while bit:
        blocks.update({k ^ bit: flip(v, "tangent", bit) for k, v in list(blocks.items())})
        bit //= 2
    blocks = [blocks[k] for k in range(shards)]
    held = bc + (shards - 1) * (bc // 2)
    direct = pieces <= 8
    cuts = pieces if direct else 1
    size = held // cuts
    piece = jax.ShapeDtypeStruct((size, bc), F32)

    def gram(*refs):
        gram_kernel(shards, cuts, bc, *refs)

    parts = call(
        gram, (shards, cuts), (piece,) * cuts, [pltpu.VMEM((held, bc), F32)], blocks
    )
    if direct:
        arrived = [parts[0]]
        for k in range(1, pieces):
            arrived.append(lax.ppermute(parts[k], "space", [(i, (i + k) % pieces) for i in range(pieces)]))
        total = call(lambda a, out: sum_kernel(a, out), (pieces,), piece, [], arrived)
        around = [total]
        for k in range(1, pieces):
            around.append(lax.ppermute(total, "space", [(i, (i + k) % pieces) for i in range(pieces)]))
        total = jnp.stack(around)
    else:
        total = lax.psum(parts[0], "space")[None]
    totals = {0: total}
    bit = shards // 2
    while bit:
        totals.update({k ^ bit: flip(v, "tangent", bit) for k, v in list(totals.items())})
        bit //= 2
    totals = [totals[k] for k in range(shards)]
    scale = 1.0 / (float(rows) * pieces)

    def solve(g_refs, x_refs, *refs):
        solve_kernel(shards, cuts, bc, scale, g_refs, x_refs, *refs)

    full = shards * bc
    out, logs = call(
        solve,
        (shards, shards),
        (jax.ShapeDtypeStruct((rows, bc), F32), jax.ShapeDtypeStruct((1, bc), F32)),
        [
            pltpu.VMEM((full, full), F32),
            pltpu.VMEM((full, BLOCK), F32),
            pltpu.VMEM((BLOCK, BLOCK), F32),
            pltpu.VMEM((held, bc), F32),
        ],
        totals + blocks,
    )
    return out, logs[0]


def lattice_rows(raw_ref, first, count):
    cells = raw_ref.shape[0]
    high = cells * TALL
    sites = [
        raw_ref[c, 0:1, :].astype(jnp.int32) * high + raw_ref[c, 1:2, :].astype(jnp.int32) + c * TALL
        for c in range(cells)
    ]
    site = jnp.concatenate(sites, axis=1)
    rows = lax.broadcasted_iota(jnp.int32, (count, site.shape[1]), 0) + first
    return jnp.where(rows == site, 1.0, 0.0).astype(BF16)


def three_parts(a):
    high, rest = a.astype(BF16), None
    rest = a - high.astype(F32)
    mid = rest.astype(BF16)
    return high, mid, (rest - mid.astype(F32)).astype(BF16)


def sort_kernel(raw_ref, count_ref, tangent_ref, state_ref, left_ref, right_ref):
    cells, comps, slots, bc = tangent_ref.shape
    high = cells * TALL
    place = lattice_rows(raw_ref, 0, high * WIDE)
    slot = lax.broadcasted_iota(jnp.int32, (slots, bc), 0)
    for comp in range(comps):
        rows = [jnp.where(slot < count_ref[c], tangent_ref[c, comp], 0.0) for c in range(cells)]
        top, low = two_parts(jnp.concatenate(rows, axis=0))
        moved = matmul(place, top, ((1,), (0,))) + matmul(place, low, ((1,), (0,)))
        state_ref[comp] = moved.reshape(WIDE, high, bc)
        near = moved.astype(BF16).reshape(WIDE, high, bc)
        if comp < 2:
            left_ref[3 * comp : 3 * comp + 3] = near[0:3]
            right_ref[3 * comp : 3 * comp + 3] = near[WIDE - 3 :]
        else:
            at = 6 + 2 * (comp - 2)
            left_ref[at : at + 2] = near[0:2]
            right_ref[at : at + 2] = near[WIDE - 2 :]


def bond(far_x, far_y, own_x, own_y, both, shift_x, shift_y):
    dx = shift_x + far_x - own_x
    dy = shift_y + far_y - own_y
    dist2 = dx * dx + dy * dy
    within = jnp.logical_and(dist2 < CUT2, both > 0.5)
    weight = jnp.where(within, 1.0, 0.0)
    safe = jnp.where(within, dist2, CUT2)
    inverse = 1.0 / safe
    inv_three = inverse * inverse * inverse
    inv_six = inv_three * inv_three
    energy = 4.0 * (inv_six - inv_three) + 1.0
    energy_1 = 4.0 * (3.0 * inv_three - 6.0 * inv_six) * inverse
    energy_2 = 4.0 * (42.0 * inv_six - 12.0 * inv_three) * inverse * inverse
    taper = 1.0 - safe * (1.0 / CUT2)
    switch = taper * taper
    switch_1 = taper * (-2.0 / CUT2)
    switch_2 = 2.0 / (CUT2 * CUT2)
    twice_1 = (energy_1 * switch + energy * switch_1) * weight * 2.0
    four_2 = (energy_2 * switch + 2.0 * energy_1 * switch_1 + energy * switch_2) * weight * 4.0
    k_xx = twice_1 + four_2 * dx * dx
    k_xy = four_2 * dx * dy
    k_yy = twice_1 + four_2 * dy * dy
    return twice_1 * dx, twice_1 * dy, (k_xx, k_xy, k_yy)


def up(a):
    return pltpu.roll(a, a.shape[0] - 1, 0)


def down(a):
    return pltpu.roll(a, 1, 0)


KICKS = tuple((0.5 if step in (0, STEPS) else 1.0) * DT for step in range(STEPS + 1))


def path_kernel(raw_ref, low_ref, high_ref, phase_ref, k_ref, lat):
    cells, _, slots = raw_ref.shape
    tall = cells * TALL
    halo = STEPS + 1
    columns = WIDE + 2 * halo
    own = lattice_rows(raw_ref, 0, WIDE * tall)
    sides = (
        (low_ref, lattice_rows(low_ref, (WIDE - halo) * tall, halo * tall), 0, halo),
        (raw_ref, own, halo, WIDE),
        (high_ref, lattice_rows(high_ref, 0, halo * tall), halo + WIDE, halo),
    )
    for ref, place, first, width in sides:
        for item in range(5):
            row = jnp.concatenate([ref[c, item : item + 1, :] for c in range(cells)], axis=1)
            wide = jnp.broadcast_to(row, (BLOCK, row.shape[1]))
            parts = three_parts(wide) if item < 4 else (wide.astype(BF16),)
            value = sum(matmul(place, part, ((1,), (1,))) for part in parts)
            lat[item, first : first + width] = value.reshape(width, tall, BLOCK)
    site = lax.broadcasted_iota(jnp.int32, (tall, BLOCK), 0)
    shift_y = jnp.where(lax.rem(site, TALL) == TALL - 1, float(TALL), 0.0)
    zero = jnp.zeros((tall, BLOCK), F32)
    for step, kick in enumerate(KICKS):
        move = DT if step < STEPS else 0.0

        def column(c, carry):
            x, y, alive, pull_x, pull_y = carry
            far_x, far_y, far_alive = lat[0, c + 1], lat[1, c + 1], lat[4, c + 1]
            crossing = jnp.logical_or(c == halo - 1, c == halo + WIDE - 1)
            shift_x = jnp.where(crossing, float(WIDE), 0.0)
            side_x, side_y, k_side = bond(far_x, far_y, x, y, alive * far_alive, shift_x, 0.0)
            over_x, over_y, k_over = bond(up(x), up(y), x, y, alive * up(alive), 0.0, shift_y)
            for a in range(3):
                k_ref[step, a, c] = k_side[a].astype(BF16)
                k_ref[step, 3 + a, c] = k_over[a].astype(BF16)
            speed_x = lat[2, c] + kick * (side_x - pull_x + over_x - down(over_x))
            speed_y = lat[3, c] + kick * (side_y - pull_y + over_y - down(over_y))
            lat[2, c], lat[3, c] = speed_x, speed_y
            if move:
                lat[0, c], lat[1, c] = x + move * speed_x, y + move * speed_y
            return far_x, far_y, far_alive, side_x, side_y

        start = (lat[0, step], lat[1, step], lat[4, step], zero, zero)
        lax.fori_loop(step, columns - 1 - step, column, start)
    for item in range(4):
        value = lat[item, halo : halo + WIDE, :, 0:TILE].reshape(WIDE * tall, TILE)
        back = sum(matmul(part, own, ((0,), (0,))) for part in three_parts(value))
        for c in range(cells):
            phase_ref[c, item : item + 1, :] = back[0:1, c * slots : (c + 1) * slots]


def tangent_kernel(raw_ref, k_ref, state_ref, low_ref, high_ref, x_ref, wide):
    cells, comps, slots, bc = x_ref.shape
    tall = cells * TALL
    halo = STEPS + 1
    columns = WIDE + 2 * halo
    for comp in range(comps):
        wide[comp, halo : halo + WIDE] = state_ref[comp]
        if comp < 2:
            wide[comp, 0:halo] = low_ref[3 * comp : 3 * comp + 3].astype(F32)
            wide[comp, halo + WIDE :] = high_ref[3 * comp : 3 * comp + 3].astype(F32)
        else:
            at = 6 + 2 * (comp - 2)
            wide[comp, 1:halo] = low_ref[at : at + 2].astype(F32)
            wide[comp, halo + WIDE : columns - 1] = high_ref[at : at + 2].astype(F32)
    zero = jnp.zeros((tall, bc), F32)

    def rounded(comp, c):
        return wide[comp, c].astype(BF16).astype(F32)

    def stretched(step, a, c):
        k = k_ref[step, a, c].astype(F32)
        return jnp.concatenate([k] * (bc // BLOCK), axis=1)

    for step, kick in enumerate(KICKS):
        move = DT if step < STEPS else 0.0

        def push(c, k0, e_x, e_y):
            k_xx, k_xy, k_yy = [stretched(step, k0 + a, c) for a in range(3)]
            return k_xx * e_x + k_xy * e_y, k_xy * e_x + k_yy * e_y

        def column(c, carry):
            x, y, pull_x, pull_y = carry
            far_x, far_y = rounded(0, c + 1), rounded(1, c + 1)
            side_x, side_y = push(c, 0, far_x - x, far_y - y)
            over_x, over_y = push(c, 3, up(x) - x, up(y) - y)
            speed_x = wide[2, c] + kick * (side_x - pull_x + over_x - down(over_x))
            speed_y = wide[3, c] + kick * (side_y - pull_y + over_y - down(over_y))
            wide[2, c], wide[3, c] = speed_x, speed_y
            if move:
                wide[0, c] = wide[0, c] + move * speed_x
                wide[1, c] = wide[1, c] + move * speed_y
            return far_x, far_y, side_x, side_y

        x, y = rounded(0, step), rounded(1, step)
        first = push(step, 0, rounded(0, step + 1) - x, rounded(1, step + 1) - y)
        start = (rounded(0, step + 1), rounded(1, step + 1)) + first
        lax.fori_loop(step + 1, columns - 1 - step, column, start)
    place = lattice_rows(raw_ref, 0, WIDE * tall)
    for comp in range(comps):
        value = wide[comp, halo : halo + WIDE].reshape(WIDE * tall, bc).astype(BF16)
        back = matmul(place, value, ((0,), (0,))).astype(BF16)
        for c in range(cells):
            x_ref[c, comp] = back[c * slots : (c + 1) * slots]


def dynamics(positions, momenta, cell_count, tangent):
    cells, comps, slots, bc = tangent.shape
    tall = cells * TALL
    columns = WIDE + 2 * (STEPS + 1)
    occupied = (lax.broadcasted_iota(jnp.int32, (cells, 1, slots), 2) < cell_count[:, None, None]).astype(F32)
    raw = jnp.concatenate([positions, momenta, occupied], axis=1)
    count = lax.axis_size("space")
    forward = [(i, (i + 1) % count) for i in range(count)]
    backward = [(b, a) for a, b in forward]
    raw_low, raw_high = lax.ppermute(raw, "space", forward), lax.ppermute(raw, "space", backward)
    halo = jax.ShapeDtypeStruct((10, tall, bc), BF16)
    vmem = pl.BlockSpec(memory_space=pltpu.VMEM)
    params = pltpu.CompilerParams(vmem_limit_bytes=48 * 1024 * 1024)
    state, left, right = pl.pallas_call(
        sort_kernel,
        out_shape=(jax.ShapeDtypeStruct((comps, WIDE, tall, bc), F32), halo, halo),
        in_specs=[vmem, pl.BlockSpec(memory_space=pltpu.SMEM), vmem],
        compiler_params=params,
    )(raw, cell_count, tangent)
    low, high = lax.ppermute(right, "space", forward), lax.ppermute(left, "space", backward)
    phase, k = pl.pallas_call(
        path_kernel,
        out_shape=(
            jax.ShapeDtypeStruct((cells, 4, slots), F32),
            jax.ShapeDtypeStruct((STEPS + 1, 6, columns, tall, BLOCK), BF16),
        ),
        scratch_shapes=[pltpu.VMEM((5, columns, tall, BLOCK), F32)],
        compiler_params=params,
        cost_estimate=pl.CostEstimate(flops=4 * 10**9, bytes_accessed=4 * 10**6, transcendentals=0),
    )(raw, raw_low, raw_high)
    x = pl.pallas_call(
        tangent_kernel,
        out_shape=jax.ShapeDtypeStruct(tangent.shape, BF16),
        scratch_shapes=[pltpu.VMEM((comps, columns, tall, bc), F32)],
        compiler_params=params,
    )(raw, k, state, low, high)
    return phase, x


def body(positions, momenta, cell_count, tangent):
    phase, x = dynamics(positions, momenta, cell_count, tangent)
    out, stretch = orthonormalize(x.reshape(-1, x.shape[3]))
    return (phase, out.reshape(x.shape), stretch)


def solution(mesh):
    placed = (
        P(("groups", "space"), None, None),
        P(("groups", "space"), None, None),
        P(("groups", "space")),
        P(("groups", "space"), None, None, "tangent"),
    )
    return jax.shard_map(
        body,
        mesh=mesh,
        in_specs=placed,
        out_specs=(
            P(("groups", "space"), None, None),
            P(("groups", "space"), None, None, "tangent"),
            P(("groups", "tangent")),
        ),
        check_vma=False,
    )
```

```python
import jax
import jax.numpy as jnp
from jax import lax
from jax.experimental import pallas as pl
from jax.experimental.pallas import tpu as pltpu
from jax.sharding import PartitionSpec as P

STEPS = 2


DT = 0.005
CUT2 = 2.0 ** (1.0 / 3.0)
WIDE, TALL = 8, 16


BLOCK = 128
TILE = 8
NEAR = 3
BF16 = jnp.bfloat16
F32 = jnp.float32


def matmul(a, b, dims):
    return lax.dot_general(a, b, (dims, ((), ())), preferred_element_type=F32)


def two_parts(a):
    high = a.astype(BF16)
    return high, (a - high.astype(F32)).astype(BF16)


def three_pass(a, b, axis_a):
    a_high, a_low = two_parts(a)
    b_high, b_low = two_parts(b)
    left = jnp.concatenate([a_high, a_high, a_low], axis=axis_a)
    right = jnp.concatenate([b_high, b_low, b_high], axis=0)
    return matmul(left, right, ((axis_a,), (0,)))


def spread(row, sublane):
    return jnp.broadcast_to(row[sublane : sublane + 1, :], row.shape)


def columns_of(tile, group):
    return [jnp.broadcast_to(tile[:, k : k + 1], tile.shape) for k in range(TILE * group, TILE * (group + 1))]


def factor_block(tiles):
    shape = tiles[0].shape
    sub = lax.broadcasted_iota(jnp.int32, shape, 0)
    lane = lax.broadcasted_iota(jnp.int32, shape, 1)
    tiles, rows_out, pivots = list(tiles), [], []
    cols = columns_of(tiles[0], 0)
    for j, tile in enumerate(tiles):
        first, more = TILE * j, j + 1 < len(tiles)
        if more:
            ahead, cols_next, ahead_next = (
                columns_of(tile, j + 1), columns_of(tiles[j + 1], j), columns_of(tiles[j + 1], j + 1)
            )
        inverse, ratio, rows = [], {}, []
        pivot = jnp.zeros(shape, F32)
        for k in range(TILE):
            top = spread(cols[k], k)
            pivot = jnp.where(sub == k, top, pivot)
            inverse.append(1.0 / top)
            for m in range(k + 1, TILE):
                ratio[k, m] = spread(cols[m], k) * inverse[k]
                cols[m] = cols[m] - cols[k] * ratio[k, m]
            rows.append(spread(tile, k) + jnp.where(lane == first + k, 1.0, 0.0))
            tile = tile - jnp.where(sub > k, cols[k] * inverse[k], 0.0) * rows[k]
            if more:
                for m in range(TILE):
                    part = spread(ahead[m], k) * inverse[k]
                    ahead[m] = ahead[m] - cols[k] * part
                    ahead_next[m] = ahead_next[m] - cols_next[k] * part
                for m in range(k + 1, TILE):
                    cols_next[m] = cols_next[m] - cols_next[k] * ratio[k, m]
                tiles[j + 1] = tiles[j + 1] - (cols_next[k] * inverse[k]) * rows[k]
        root = lax.rsqrt(pivot)
        unit = jnp.where(lane < sub + first, tile, jnp.where(lane == sub + first, 1.0, 0.0)) * root
        rows_out.append(unit)
        near = min(j + 1 + NEAR, len(tiles))
        if near < len(tiles):
            scaled = jnp.where(lane < first + TILE, unit, tile * root)
            high, low = [part.astype(F32) for part in two_parts(scaled)]
            left = jnp.concatenate([high, high, low], axis=0)[:, TILE * near :]
            right = jnp.concatenate([high, low, high], axis=0)
            update = matmul(left.astype(BF16), right.astype(BF16), ((0,), (0,)))
            group = jnp.logical_and(lane >= first, lane < first + TILE)
            for i in range(near, len(tiles)):
                at = TILE * (i - near)
                tiles[i] = jnp.where(group, 0.0, tiles[i]) - update[at : at + TILE, :]
        for i in range(j + 2, near):
            low, below = columns_of(tiles[i], j), tiles[i]
            for k in range(TILE):
                for m in range(k + 1, TILE):
                    low[m] = low[m] - low[k] * ratio[k, m]
                below = below - (low[k] * inverse[k]) * rows[k]
            tiles[i] = below
        pivots.append(pivot)
        if more:
            cols = ahead_next
    return rows_out, pivots


def eliminate(total, work, pivots, small):
    def one_block(step, carry):
        top = pl.multiple_of(step * BLOCK, BLOCK)
        own = pl.ds(top, BLOCK)
        tiles = [work[pl.ds(top + TILE * i, TILE), own] for i in range(BLOCK // TILE)]
        rows_out, pivot_tiles = factor_block(tiles)
        for i in range(BLOCK // TILE):
            pivots[pl.ds(top + TILE * i, TILE), :] = pivot_tiles[i]
            small[TILE * i : TILE * (i + 1), :] = rows_out[i]
        inverse = small[...]
        work[own, :] = three_pass(inverse, work[own, :], 1)
        work[own, own] = inverse
        for now in range(total - 1):

            @pl.when(step == now)
            def _():
                here, rest = slice(now * BLOCK, (now + 1) * BLOCK), slice((now + 1) * BLOCK, total * BLOCK)
                work[rest, here] = jnp.zeros(((total - 1 - now) * BLOCK, BLOCK), F32)
                work[rest, :] = work[rest, :] - three_pass(work[here, rest], work[here, :], 0)

        return carry

    lax.fori_loop(0, total, one_block, 0)


def share_pair(k, me, half, x_own, x_far, out_ref, rows):
    lower = me < (me ^ k)

    @pl.when(lower)
    def _():
        out_ref[rows, :] = matmul(x_own[:, 0:half], x_far[...], ((0,), (0,)))

    @pl.when(jnp.logical_not(lower))
    def _():
        out_ref[rows, :] = matmul(x_far[:, half:], x_own[...], ((0,), (0,)))


def deal(part, out_refs):
    size, pieces = out_refs[0].shape[0], len(out_refs)
    for k in range(pieces):
        start = pl.multiple_of(lax.rem(lax.axis_index("space") + k, pieces) * size, 8)
        out_refs[k][...] = part[pl.ds(start, size), :]


def near_gram_kernel(x_refs, out_refs, part):
    me = lax.axis_index("tangent")
    half = x_refs[0].shape[1] // 2
    quarter = half // 2
    own = x_refs[0][...]
    part[0:half, :] = matmul(own[:, 0:half], own, ((0,), (0,)))
    last = matmul(own[:, half:], own[:, half:], ((0,), (0,)))
    part[half : half + quarter, 0:half] = last[0:quarter]
    part[half : half + quarter, half:] = last[quarter:]
    for k in range(1, len(x_refs)):
        at = half + quarter + (k - 1) * half
        share_pair(k, me, half, x_refs[0], x_refs[k], part, slice(at, at + half))
    deal(part, out_refs)


def far_gram_kernel(x_own, x_refs, out_refs, part):
    bc = x_own[0].shape[1]
    for k in range(len(x_refs)):
        part[k * bc : (k + 1) * bc, :] = matmul(x_refs[k][...], x_own[0][...], ((0,), (0,)))
    deal(part, out_refs)


def sum_kernel(in_refs, out_ref):
    total = in_refs[0][...]
    for ref in in_refs[1:]:
        total = total + ref[...]
    out_ref[...] = total


def collect(g_ref, scale, part):
    pieces, size = g_ref.shape[0], g_ref.shape[1]
    for j in range(pieces):
        start = pl.multiple_of(lax.rem(lax.axis_index("space") + pieces - j, pieces) * size, 8)
        part[pl.ds(start, size), :] = g_ref[j] * scale


def place_pairs(peer, count, offset, part, work):
    bc = part.shape[1]
    half = bc // 2
    for j in range(1, count):
        other = peer ^ j
        low, high = jnp.minimum(peer, other), jnp.maximum(peer, other)
        top = pl.multiple_of(low * bc + jnp.where(peer == high, half, 0), half)
        at = offset + (j - 1) * half
        work[pl.ds(top, half), pl.ds(pl.multiple_of(high * bc, BLOCK), bc)] = part[at : at + half, :]


def near_blocks(g_refs, upper, scale, part, work):
    me = lax.axis_index("tangent")
    shards = len(g_refs)
    inner = shards // 2
    bc = part.shape[1]
    half = bc // 2
    quarter = half // 2
    for k in range(shards):
        same_half = (me < inner) if (k < inner) != upper else (me >= inner)

        @pl.when(same_half)
        def _():
            peer = (me ^ k) & (inner - 1)
            collect(g_refs[k], scale, part)
            top = pl.multiple_of(peer * bc, BLOCK)
            work[pl.ds(top, half), pl.ds(top, bc)] = part[0:half, :]
            if half % BLOCK:
                full = part[0:half, half:]
                block = jnp.concatenate([part[half : half + quarter, 0:half], part[half : half + quarter, half:]], axis=0)
                work[pl.ds(top + half, half), pl.ds(top, bc)] = jnp.concatenate([full.T, block], axis=1)
            else:
                right = pl.ds(pl.multiple_of(top + half, BLOCK), half)
                work[pl.ds(top + half, quarter), right] = part[half : half + quarter, 0:half]
                work[pl.ds(top + half + quarter, quarter), right] = part[half : half + quarter, half:]
            place_pairs(peer, inner, half + quarter, part, work)


def log_rows(pivots, log_ref):
    eye = lax.broadcasted_iota(jnp.int32, (BLOCK, BLOCK), 0) == lax.broadcasted_iota(jnp.int32, (BLOCK, BLOCK), 1)
    for a in range(pivots.shape[0] // BLOCK):
        block = pivots[a * BLOCK : (a + 1) * BLOCK, :]
        log_ref[:, a * BLOCK : (a + 1) * BLOCK] = 0.5 * jnp.log(
            jnp.sum(jnp.where(eye, block, 0.0), axis=0, keepdims=True)
        )


def lower_blocks(matrix):
    row_block = lax.broadcasted_iota(jnp.int32, matrix.shape, 0) // BLOCK
    col_block = lax.broadcasted_iota(jnp.int32, matrix.shape, 1) // BLOCK
    return jnp.where(row_block >= col_block, matrix, 0.0)


def first_kernel(scale, g_refs, inverse_ref, log_ref, pivots, small, part):
    near_blocks(g_refs, False, scale, part, inverse_ref)
    eliminate(inverse_ref.shape[0] // BLOCK, inverse_ref, pivots, small)
    inverse_ref[...] = lower_blocks(inverse_ref[...])
    log_rows(pivots, log_ref)


def second_kernel(
    scale, near_refs, far_refs, x_refs, first_ref, first_log, out_ref, log_ref,
    work, cross, product, mine, logs, pivots, small, near_part, far_part,
):
    me = lax.axis_index("tangent")
    shards = len(x_refs)
    inner = shards // 2
    bc = out_ref.shape[1]
    full = work.shape[0]
    near_blocks(near_refs, True, scale, near_part, work)

    @pl.when(me < inner)
    def _():
        cross[...] = jnp.zeros(cross.shape, F32)

    @pl.when(me >= inner)
    def _():
        for k in range(inner):
            collect(far_refs[k], scale, far_part)
            cols = pl.ds(pl.multiple_of((me ^ k) * bc - full, BLOCK), bc)
            for j in range(inner):
                rows = pl.ds(pl.multiple_of((me ^ k ^ (j + inner)) * bc, BLOCK), bc)
                cross[rows, cols] = far_part[j * bc : (j + 1) * bc, :]

    cross[...] = three_pass(first_ref[...], cross[...], 1)
    work[...] = work[...] - three_pass(cross[...], cross[...], 0)
    product[...] = three_pass(cross[...], first_ref[...], 0)
    eliminate(full // BLOCK, work, pivots, small)
    log_rows(pivots, logs)
    top = pl.multiple_of((me & (inner - 1)) * bc, BLOCK)
    rows = pl.ds(top, bc)

    @pl.when(me < inner)
    def _():
        mine[:, 0:full] = first_ref[rows, :]
        mine[:, full:] = jnp.zeros((bc, full), F32)
        log_ref[...] = first_log[:, rows]

    @pl.when(me >= inner)
    def _():
        row_block = (lax.broadcasted_iota(jnp.int32, (bc, full), 0) + top) // BLOCK
        col_block = lax.broadcasted_iota(jnp.int32, (bc, full), 1) // BLOCK
        own = jnp.where(row_block >= col_block, work[rows, :], 0.0)
        mine[:, full:] = own
        mine[:, 0:full] = -three_pass(own, product[...], 1)
        log_ref[...] = logs[:, rows]

    def times(x_ref, peer):
        high, low = two_parts(mine[:, pl.ds(pl.multiple_of(peer * bc, BLOCK), bc)])
        return matmul(x_ref[...], high, ((1,), (1,))) + matmul(x_ref[...], low, ((1,), (1,)))

    out_ref[...] = times(x_refs[0], me)
    for k in range(1, shards):
        peer = me ^ k

        @pl.when(peer < me)
        def _():
            out_ref[...] += times(x_refs[k], peer)


def call(kernel, counts, out_shapes, scratch, operands, cost=None, after=()):
    inputs, waits = len(operands), len(after)

    def unpacked(*refs):
        refs = refs[:inputs] + refs[inputs + waits :]
        groups, at = [], 0
        for count in counts:
            groups.append(refs[at : at + count])
            at += count
        kernel(*groups, *refs[at:])

    return pl.pallas_call(
        unpacked,
        out_shape=out_shapes,
        in_specs=[pl.BlockSpec(memory_space=pltpu.VMEM)] * inputs + [pl.BlockSpec(memory_space=pl.ANY)] * waits,
        scratch_shapes=scratch,
        cost_estimate=cost,
        compiler_params=pltpu.CompilerParams(vmem_limit_bytes=48 * 1024 * 1024),
    )(*operands, *after)


def flip(array, axis, bit):
    return lax.ppermute(array, axis, [(i, i ^ bit) for i in range(lax.axis_size(axis))])


def flips(blocks, bits):
    for bit in bits:
        blocks = {**blocks, **{k ^ bit: flip(v, "tangent", bit) for k, v in blocks.items()}}
    return blocks


def scatter(parts, count):
    if len(parts) == 1:
        return [lax.psum(parts[0], "space")]
    arrived = [parts[0]]
    for k in range(1, count):
        arrived.append(lax.ppermute(parts[k], "space", [(i, (i + k) % count) for i in range(count)]))
    return arrived


def added(arrived, after=()):
    shape = jax.ShapeDtypeStruct(arrived[0].shape, F32)
    return call(sum_kernel, (len(arrived),), shape, [], arrived, after=after)


def gather(total, count, cuts):
    around = [total]
    for k in range(1, cuts):
        around.append(lax.ppermute(total, "space", [(i, (i + k) % count) for i in range(count)]))
    return around


def orthonormalize(x):
    shards, count = lax.axis_size("tangent"), lax.axis_size("space")
    rows, bc = x.shape
    half, inner = bc // 2, shards // 2
    cuts = count if count <= 8 else 1
    bits = [1 << b for b in reversed(range(inner.bit_length() - 1))]
    scale = 1.0 / (float(rows) * count)
    near_rows, far_rows = half + half // 2 + (inner - 1) * half, inner * bc

    def dealt(held):
        return (jax.ShapeDtypeStruct((held // cuts, bc), F32),) * cuts

    far_own = flip(x, "tangent", inner)
    near_x = flips({0: x}, bits)
    near_x = [near_x[k] for k in range(inner)]
    near = call(near_gram_kernel, (inner, cuts), dealt(near_rows), [pltpu.VMEM((near_rows, bc), F32)], near_x)
    near = added(scatter(near, count))
    around = gather(near, count, cuts)
    far_x = flips({0: lax.optimization_barrier((far_own, near))[0]}, bits)
    far_x = [far_x[k] for k in range(inner)]
    far = call(
        far_gram_kernel,
        (1, inner, cuts),
        dealt(far_rows),
        [pltpu.VMEM((far_rows, bc), F32)],
        [x] + far_x,
        after=[near],
    )
    near = jnp.stack(lax.optimization_barrier((around, far[0]))[0])
    far = added(scatter(far, count), after=[near])
    far_around = gather(far, count, cuts)
    near = flips({0: near}, [inner])
    near[inner] = lax.optimization_barrier((near[inner], far))[0]
    near = flips(near, bits)
    near = [near[k] for k in range(shards)]
    full = inner * bc
    square, column = pltpu.VMEM((full, full), F32), pltpu.VMEM((full, BLOCK), F32)
    block, near_part = pltpu.VMEM((BLOCK, BLOCK), F32), pltpu.VMEM((near_rows, bc), F32)
    first, first_log = call(
        lambda *refs: first_kernel(scale, *refs),
        (shards,),
        (jax.ShapeDtypeStruct((full, full), F32), jax.ShapeDtypeStruct((1, full), F32)),
        [column, block, near_part],
        near,
        cost=pl.CostEstimate(flops=16 * 10**9, bytes_accessed=4 * 10**6, transcendentals=0),
    )
    far_around = lax.optimization_barrier((far_around, first_log))[0]
    far = flips({0: jnp.stack(far_around)}, bits)
    far = [far[k] for k in range(inner)]
    out, logs = call(
        lambda *refs: second_kernel(scale, *refs),
        (shards, inner, shards),
        (jax.ShapeDtypeStruct((rows, bc), F32), jax.ShapeDtypeStruct((1, bc), F32)),
        [
            square, square, square, pltpu.VMEM((bc, 2 * full), F32), pltpu.VMEM((1, full), F32),
            column, block, near_part, pltpu.VMEM((far_rows, bc), F32),
        ],
        near + far + near_x + far_x + [first, first_log],
    )
    return out, logs[0]


def lattice_rows(raw_ref, first, count):
    cells = raw_ref.shape[0]
    high = cells * TALL
    sites = [
        raw_ref[c, 0:1, :].astype(jnp.int32) * high + raw_ref[c, 1:2, :].astype(jnp.int32) + c * TALL
        for c in range(cells)
    ]
    site = jnp.concatenate(sites, axis=1)
    rows = lax.broadcasted_iota(jnp.int32, (count, site.shape[1]), 0) + first
    return jnp.where(rows == site, 1.0, 0.0).astype(BF16)


def three_parts(a):
    high, rest = a.astype(BF16), None
    rest = a - high.astype(F32)
    mid = rest.astype(BF16)
    return high, mid, (rest - mid.astype(F32)).astype(BF16)


def sort_kernel(raw_ref, count_ref, tangent_ref, state_ref, left_ref, right_ref):
    cells, comps, slots, bc = tangent_ref.shape
    high = cells * TALL
    place = lattice_rows(raw_ref, 0, high * WIDE)
    slot = lax.broadcasted_iota(jnp.int32, (slots, bc), 0)
    for comp in range(comps):
        rows = [jnp.where(slot < count_ref[c], tangent_ref[c, comp], 0.0) for c in range(cells)]
        top, low = two_parts(jnp.concatenate(rows, axis=0))
        moved = matmul(place, top, ((1,), (0,))) + matmul(place, low, ((1,), (0,)))
        state_ref[comp] = moved.reshape(WIDE, high, bc)
        near = moved.astype(BF16).reshape(WIDE, high, bc)
        if comp < 2:
            left_ref[3 * comp : 3 * comp + 3] = near[0:3]
            right_ref[3 * comp : 3 * comp + 3] = near[WIDE - 3 :]
        else:
            at = 6 + 2 * (comp - 2)
            left_ref[at : at + 2] = near[0:2]
            right_ref[at : at + 2] = near[WIDE - 2 :]


def bond(far_x, far_y, own_x, own_y, both, shift_x, shift_y):
    dx = shift_x + far_x - own_x
    dy = shift_y + far_y - own_y
    dist2 = dx * dx + dy * dy
    within = jnp.logical_and(dist2 < CUT2, both > 0.5)
    weight = jnp.where(within, 1.0, 0.0)
    safe = jnp.where(within, dist2, CUT2)
    inverse = 1.0 / safe
    inv_three = inverse * inverse * inverse
    inv_six = inv_three * inv_three
    energy = 4.0 * (inv_six - inv_three) + 1.0
    energy_1 = 4.0 * (3.0 * inv_three - 6.0 * inv_six) * inverse
    energy_2 = 4.0 * (42.0 * inv_six - 12.0 * inv_three) * inverse * inverse
    taper = 1.0 - safe * (1.0 / CUT2)
    switch = taper * taper
    switch_1 = taper * (-2.0 / CUT2)
    switch_2 = 2.0 / (CUT2 * CUT2)
    twice_1 = (energy_1 * switch + energy * switch_1) * weight * 2.0
    four_2 = (energy_2 * switch + 2.0 * energy_1 * switch_1 + energy * switch_2) * weight * 4.0
    k_xx = twice_1 + four_2 * dx * dx
    k_xy = four_2 * dx * dy
    k_yy = twice_1 + four_2 * dy * dy
    return twice_1 * dx, twice_1 * dy, (k_xx, k_xy, k_yy)


def up(a):
    return pltpu.roll(a, a.shape[0] - 1, 0)


def down(a):
    return pltpu.roll(a, 1, 0)


KICKS = tuple((0.5 if step in (0, STEPS) else 1.0) * DT for step in range(STEPS + 1))


def path_kernel(raw_ref, low_ref, high_ref, phase_ref, k_ref, lat):
    cells, _, slots = raw_ref.shape
    tall = cells * TALL
    halo = STEPS + 1
    columns = WIDE + 2 * halo
    own = lattice_rows(raw_ref, 0, WIDE * tall)
    sides = (
        (low_ref, lattice_rows(low_ref, (WIDE - halo) * tall, halo * tall), 0, halo),
        (raw_ref, own, halo, WIDE),
        (high_ref, lattice_rows(high_ref, 0, halo * tall), halo + WIDE, halo),
    )
    for ref, place, first, width in sides:
        for item in range(5):
            row = jnp.concatenate([ref[c, item : item + 1, :] for c in range(cells)], axis=1)
            wide = jnp.broadcast_to(row, (BLOCK, row.shape[1]))
            parts = three_parts(wide) if item < 4 else (wide.astype(BF16),)
            value = sum(matmul(place, part, ((1,), (1,))) for part in parts)
            lat[item, first : first + width] = value.reshape(width, tall, BLOCK)
    site = lax.broadcasted_iota(jnp.int32, (tall, BLOCK), 0)
    shift_y = jnp.where(lax.rem(site, TALL) == TALL - 1, float(TALL), 0.0)
    zero = jnp.zeros((tall, BLOCK), F32)
    for step, kick in enumerate(KICKS):
        move = DT if step < STEPS else 0.0

        def column(c, carry):
            x, y, alive, pull_x, pull_y = carry
            far_x, far_y, far_alive = lat[0, c + 1], lat[1, c + 1], lat[4, c + 1]
            crossing = jnp.logical_or(c == halo - 1, c == halo + WIDE - 1)
            shift_x = jnp.where(crossing, float(WIDE), 0.0)
            side_x, side_y, k_side = bond(far_x, far_y, x, y, alive * far_alive, shift_x, 0.0)
            over_x, over_y, k_over = bond(up(x), up(y), x, y, alive * up(alive), 0.0, shift_y)
            for a in range(3):
                k_ref[step, a, c] = k_side[a].astype(BF16)
                k_ref[step, 3 + a, c] = k_over[a].astype(BF16)
            speed_x = lat[2, c] + kick * (side_x - pull_x + over_x - down(over_x))
            speed_y = lat[3, c] + kick * (side_y - pull_y + over_y - down(over_y))
            lat[2, c], lat[3, c] = speed_x, speed_y
            if move:
                lat[0, c], lat[1, c] = x + move * speed_x, y + move * speed_y
            return far_x, far_y, far_alive, side_x, side_y

        start = (lat[0, step], lat[1, step], lat[4, step], zero, zero)
        lax.fori_loop(step, columns - 1 - step, column, start)
    for item in range(4):
        value = lat[item, halo : halo + WIDE, :, 0:TILE].reshape(WIDE * tall, TILE)
        back = sum(matmul(part, own, ((0,), (0,))) for part in three_parts(value))
        for c in range(cells):
            phase_ref[c, item : item + 1, :] = back[0:1, c * slots : (c + 1) * slots]


def tangent_kernel(raw_ref, k_ref, state_ref, low_ref, high_ref, x_ref, wide):
    cells, comps, slots, bc = x_ref.shape
    tall = cells * TALL
    halo = STEPS + 1
    columns = WIDE + 2 * halo
    for comp in range(comps):
        wide[comp, halo : halo + WIDE] = state_ref[comp]
        if comp < 2:
            wide[comp, 0:halo] = low_ref[3 * comp : 3 * comp + 3].astype(F32)
            wide[comp, halo + WIDE :] = high_ref[3 * comp : 3 * comp + 3].astype(F32)
        else:
            at = 6 + 2 * (comp - 2)
            wide[comp, 1:halo] = low_ref[at : at + 2].astype(F32)
            wide[comp, halo + WIDE : columns - 1] = high_ref[at : at + 2].astype(F32)
    zero = jnp.zeros((tall, bc), F32)

    def rounded(comp, c):
        return wide[comp, c].astype(BF16).astype(F32)

    def stretched(step, a, c):
        k = k_ref[step, a, c].astype(F32)
        return jnp.concatenate([k] * (bc // BLOCK), axis=1)

    for step, kick in enumerate(KICKS):
        move = DT if step < STEPS else 0.0

        def push(c, k0, e_x, e_y):
            k_xx, k_xy, k_yy = [stretched(step, k0 + a, c) for a in range(3)]
            return k_xx * e_x + k_xy * e_y, k_xy * e_x + k_yy * e_y

        def column(c, carry):
            x, y, pull_x, pull_y = carry
            far_x, far_y = rounded(0, c + 1), rounded(1, c + 1)
            side_x, side_y = push(c, 0, far_x - x, far_y - y)
            over_x, over_y = push(c, 3, up(x) - x, up(y) - y)
            speed_x = wide[2, c] + kick * (side_x - pull_x + over_x - down(over_x))
            speed_y = wide[3, c] + kick * (side_y - pull_y + over_y - down(over_y))
            wide[2, c], wide[3, c] = speed_x, speed_y
            if move:
                wide[0, c] = wide[0, c] + move * speed_x
                wide[1, c] = wide[1, c] + move * speed_y
            return far_x, far_y, side_x, side_y

        x, y = rounded(0, step), rounded(1, step)
        first = push(step, 0, rounded(0, step + 1) - x, rounded(1, step + 1) - y)
        start = (rounded(0, step + 1), rounded(1, step + 1)) + first
        lax.fori_loop(step + 1, columns - 1 - step, column, start)
    place = lattice_rows(raw_ref, 0, WIDE * tall)
    for comp in range(comps):
        value = wide[comp, halo : halo + WIDE].reshape(WIDE * tall, bc).astype(BF16)
        back = matmul(place, value, ((0,), (0,))).astype(BF16)
        for c in range(cells):
            x_ref[c, comp] = back[c * slots : (c + 1) * slots]


def dynamics(positions, momenta, cell_count, tangent):
    cells, comps, slots, bc = tangent.shape
    tall = cells * TALL
    columns = WIDE + 2 * (STEPS + 1)
    occupied = (lax.broadcasted_iota(jnp.int32, (cells, 1, slots), 2) < cell_count[:, None, None]).astype(F32)
    raw = jnp.concatenate([positions, momenta, occupied], axis=1)
    count = lax.axis_size("space")
    forward = [(i, (i + 1) % count) for i in range(count)]
    backward = [(b, a) for a, b in forward]
    raw_low, raw_high = lax.ppermute(raw, "space", forward), lax.ppermute(raw, "space", backward)
    halo = jax.ShapeDtypeStruct((10, tall, bc), BF16)
    vmem = pl.BlockSpec(memory_space=pltpu.VMEM)
    params = pltpu.CompilerParams(vmem_limit_bytes=48 * 1024 * 1024)
    state, left, right = pl.pallas_call(
        sort_kernel,
        out_shape=(jax.ShapeDtypeStruct((comps, WIDE, tall, bc), F32), halo, halo),
        in_specs=[vmem, pl.BlockSpec(memory_space=pltpu.SMEM), vmem],
        compiler_params=params,
    )(raw, cell_count, tangent)
    low, high = lax.ppermute(right, "space", forward), lax.ppermute(left, "space", backward)
    phase, k = pl.pallas_call(
        path_kernel,
        out_shape=(
            jax.ShapeDtypeStruct((cells, 4, slots), F32),
            jax.ShapeDtypeStruct((STEPS + 1, 6, columns, tall, BLOCK), BF16),
        ),
        scratch_shapes=[pltpu.VMEM((5, columns, tall, BLOCK), F32)],
        compiler_params=params,
        cost_estimate=pl.CostEstimate(flops=4 * 10**9, bytes_accessed=4 * 10**6, transcendentals=0),
    )(raw, raw_low, raw_high)
    x = pl.pallas_call(
        tangent_kernel,
        out_shape=jax.ShapeDtypeStruct(tangent.shape, BF16),
        scratch_shapes=[pltpu.VMEM((comps, columns, tall, bc), F32)],
        compiler_params=params,
    )(raw, k, state, low, high)
    return phase, x


def body(positions, momenta, cell_count, tangent):
    phase, x = dynamics(positions, momenta, cell_count, tangent)
    out, stretch = orthonormalize(x.reshape(-1, x.shape[3]))
    return (phase, out.reshape(x.shape), stretch)


def solution(mesh):
    placed = (
        P(("groups", "space"), None, None),
        P(("groups", "space"), None, None),
        P(("groups", "space")),
        P(("groups", "space"), None, None, "tangent"),
    )
    return jax.shard_map(
        body,
        mesh=mesh,
        in_specs=placed,
        out_specs=(
            P(("groups", "space"), None, None),
            P(("groups", "space"), None, None, "tangent"),
            P(("groups", "tangent")),
        ),
        check_vma=False,
    )
```

```python
import jax
import jax.numpy as jnp
from jax import lax
from jax.experimental import pallas as pl
from jax.experimental.pallas import tpu as pltpu
from jax.sharding import PartitionSpec as P

STEPS = 2


DT = 0.005
CUT2 = 2.0 ** (1.0 / 3.0)
WIDE, TALL, ITEMS = 8, 16, 5


BLOCK = 128
TILE = 8
NEAR = 3
BF16 = jnp.bfloat16
F32 = jnp.float32


def matmul(a, b, dims):
    return lax.dot_general(a, b, (dims, ((), ())), preferred_element_type=F32)


def two_parts(a):
    high = a.astype(BF16)
    return high, (a - high.astype(F32)).astype(BF16)


def three_pass(a, b, axis_a):
    a_high, a_low = two_parts(a)
    b_high, b_low = two_parts(b)
    left = jnp.concatenate([a_high, a_high, a_low], axis=axis_a)
    right = jnp.concatenate([b_high, b_low, b_high], axis=0)
    return matmul(left, right, ((axis_a,), (0,)))


def spread(row, sublane):
    return jnp.broadcast_to(row[sublane : sublane + 1, :], row.shape)


def columns_of(tile, group):
    return [jnp.broadcast_to(tile[:, k : k + 1], tile.shape) for k in range(TILE * group, TILE * (group + 1))]


def factor_block(tiles):
    shape = tiles[0].shape
    sub = lax.broadcasted_iota(jnp.int32, shape, 0)
    lane = lax.broadcasted_iota(jnp.int32, shape, 1)
    tiles, rows_out, pivots = list(tiles), [], []
    cols = columns_of(tiles[0], 0)
    for j, tile in enumerate(tiles):
        first, more = TILE * j, j + 1 < len(tiles)
        if more:
            ahead, cols_next, ahead_next = (
                columns_of(tile, j + 1), columns_of(tiles[j + 1], j), columns_of(tiles[j + 1], j + 1)
            )
        inverse, ratio, rows = [], {}, []
        pivot = jnp.zeros(shape, F32)
        for k in range(TILE):
            top = spread(cols[k], k)
            pivot = jnp.where(sub == k, top, pivot)
            inverse.append(1.0 / top)
            for m in range(k + 1, TILE):
                ratio[k, m] = spread(cols[m], k) * inverse[k]
                cols[m] = cols[m] - cols[k] * ratio[k, m]
            rows.append(spread(tile, k) + jnp.where(lane == first + k, 1.0, 0.0))
            tile = tile - jnp.where(sub > k, cols[k] * inverse[k], 0.0) * rows[k]
            if more:
                for m in range(TILE):
                    part = spread(ahead[m], k) * inverse[k]
                    ahead[m] = ahead[m] - cols[k] * part
                    ahead_next[m] = ahead_next[m] - cols_next[k] * part
                for m in range(k + 1, TILE):
                    cols_next[m] = cols_next[m] - cols_next[k] * ratio[k, m]
                tiles[j + 1] = tiles[j + 1] - (cols_next[k] * inverse[k]) * rows[k]
        root = lax.rsqrt(pivot)
        unit = jnp.where(lane < sub + first, tile, jnp.where(lane == sub + first, 1.0, 0.0)) * root
        rows_out.append(unit)
        near = min(j + 1 + NEAR, len(tiles))
        if near < len(tiles):
            scaled = jnp.where(lane < first + TILE, unit, tile * root)
            high, low = [part.astype(F32) for part in two_parts(scaled)]
            left = jnp.concatenate([high, high, low], axis=0)[:, TILE * near :]
            right = jnp.concatenate([high, low, high], axis=0)
            update = matmul(left.astype(BF16), right.astype(BF16), ((0,), (0,)))
            group = jnp.logical_and(lane >= first, lane < first + TILE)
            for i in range(near, len(tiles)):
                at = TILE * (i - near)
                tiles[i] = jnp.where(group, 0.0, tiles[i]) - update[at : at + TILE, :]
        for i in range(j + 2, near):
            low, below = columns_of(tiles[i], j), tiles[i]
            for k in range(TILE):
                for m in range(k + 1, TILE):
                    low[m] = low[m] - low[k] * ratio[k, m]
                below = below - (low[k] * inverse[k]) * rows[k]
            tiles[i] = below
        pivots.append(pivot)
        if more:
            cols = ahead_next
    return rows_out, pivots


def eliminate(total, work, pivots):
    size = total * BLOCK
    part = [slice(i * BLOCK, (i + 1) * BLOCK) for i in range(total)]
    for step in range(total):
        own, rest = part[step], slice((step + 1) * BLOCK, size)
        top = step * BLOCK
        tiles = [work[top + TILE * i : top + TILE * (i + 1), own] for i in range(BLOCK // TILE)]
        rows_out, pivot_tiles = factor_block(tiles)
        for i in range(BLOCK // TILE):
            pivots[top + TILE * i : top + TILE * (i + 1), :] = pivot_tiles[i]
        inverse = jnp.concatenate(rows_out, axis=0)
        if step + 1 < total:
            after = part[step + 1]
            across = three_pass(inverse, work[own, after], 1)
            work[after, after] = work[after, after] - three_pass(across, across, 0)
            work[own, after] = across
            if step + 2 < total:
                last = slice((step + 2) * BLOCK, size)
                beyond = three_pass(inverse, work[own, last], 1)
                work[own, last] = beyond
                work[after, last] = work[after, last] - three_pass(across, beyond, 0)
                work[last, last] = work[last, last] - three_pass(beyond, beyond, 0)
        if step:
            before = slice(0, top)
            work[own, before] = three_pass(inverse, work[own, before], 1)
            if step + 1 < total:
                work[rest, before] = work[rest, before] - three_pass(work[own, rest], work[own, before], 0)
        work[own, own] = inverse
        if step + 1 < total:
            work[rest, own] = -three_pass(work[own, rest], inverse, 0)


def share_pair(k, me, half, x_own, x_far, out_ref, rows):
    lower = me < (me ^ k)

    @pl.when(lower)
    def _():
        out_ref[rows, :] = matmul(x_own[:, 0:half], x_far[...], ((0,), (0,)))

    @pl.when(jnp.logical_not(lower))
    def _():
        out_ref[rows, :] = matmul(x_far[:, half:], x_own[...], ((0,), (0,)))


def deal(part, out_refs):
    size, pieces = out_refs[0].shape[0], len(out_refs)
    for k in range(pieces):
        start = pl.multiple_of(lax.rem(lax.axis_index("space") + k, pieces) * size, 8)
        out_refs[k][...] = part[pl.ds(start, size), :]


def near_gram_kernel(x_refs, out_refs, part):
    me = lax.axis_index("tangent")
    half = x_refs[0].shape[1] // 2
    quarter = half // 2
    own = x_refs[0][...]
    part[0:half, :] = matmul(own[:, 0:half], own, ((0,), (0,)))
    last = matmul(own[:, half:], own[:, half:], ((0,), (0,)))
    part[half : half + quarter, 0:half] = last[0:quarter]
    part[half : half + quarter, half:] = last[quarter:]
    for k in range(1, len(x_refs)):
        at = half + quarter + (k - 1) * half
        share_pair(k, me, half, x_refs[0], x_refs[k], part, slice(at, at + half))
    deal(part, out_refs)


def far_gram_kernel(x_own, x_refs, out_refs, part):
    bc = x_own[0].shape[1]
    for k in range(len(x_refs)):
        part[k * bc : (k + 1) * bc, :] = matmul(x_refs[k][...], x_own[0][...], ((0,), (0,)))
    deal(part, out_refs)


def sum_kernel(in_refs, out_ref):
    total = in_refs[0][...]
    for ref in in_refs[1:]:
        total = total + ref[...]
    out_ref[...] = total


def collect(g_ref, scale, part):
    pieces = g_ref.shape[0]
    size = part.shape[0] // pieces
    for j in range(pieces):
        start = pl.multiple_of(lax.rem(lax.axis_index("space") + pieces - j, pieces) * size, 8)
        part[pl.ds(start, size), :] = g_ref[j] * scale


def place_pairs(peer, count, offset, part, work):
    bc = part.shape[1]
    half = bc // 2
    for j in range(1, count):
        other = peer ^ j
        low, high = jnp.minimum(peer, other), jnp.maximum(peer, other)
        top = pl.multiple_of(low * bc + jnp.where(peer == high, half, 0), half)
        at = offset + (j - 1) * half
        work[pl.ds(top, half), pl.ds(pl.multiple_of(high * bc, BLOCK), bc)] = part[at : at + half, :]


def near_blocks(peer, part, work):
    bc = part.shape[1]
    half = bc // 2
    quarter = half // 2
    top = pl.multiple_of(peer * bc, BLOCK)
    work[pl.ds(top, half), pl.ds(top, bc)] = part[0:half, :]
    if half % BLOCK:
        full = part[0:half, half:]
        block = jnp.concatenate([part[half : half + quarter, 0:half], part[half : half + quarter, half:]], axis=0)
        work[pl.ds(top + half, half), pl.ds(top, bc)] = jnp.concatenate([full.T, block], axis=1)
    else:
        right = pl.ds(pl.multiple_of(top + half, BLOCK), half)
        work[pl.ds(top + half, quarter), right] = part[half : half + quarter, 0:half]
        work[pl.ds(top + half + quarter, quarter), right] = part[half : half + quarter, half:]
    place_pairs(peer, work.shape[0] // bc, half + quarter, part, work)


def log_rows(pivots, log_ref):
    eye = lax.broadcasted_iota(jnp.int32, (BLOCK, BLOCK), 0) == lax.broadcasted_iota(jnp.int32, (BLOCK, BLOCK), 1)
    for a in range(pivots.shape[0] // BLOCK):
        block = pivots[a * BLOCK : (a + 1) * BLOCK, :]
        log_ref[:, a * BLOCK : (a + 1) * BLOCK] = 0.5 * jnp.log(
            jnp.sum(jnp.where(eye, block, 0.0), axis=0, keepdims=True)
        )


def lower_blocks(matrix):
    row_block = lax.broadcasted_iota(jnp.int32, matrix.shape, 0) // BLOCK
    col_block = lax.broadcasted_iota(jnp.int32, matrix.shape, 1) // BLOCK
    return jnp.where(row_block >= col_block, matrix, 0.0)


def first_kernel(scale, g_refs, inverse_ref, log_ref, pivots, part):
    me = lax.axis_index("tangent")
    inner = len(g_refs) // 2
    for k in range(2 * inner):

        @pl.when((me < inner) == (k < inner))
        def _():
            collect(g_refs[k], scale, part)
            near_blocks((me ^ k) & (inner - 1), part, inverse_ref)

    eliminate(inverse_ref.shape[0] // BLOCK, inverse_ref, pivots)
    inverse_ref[...] = lower_blocks(inverse_ref[...])
    log_rows(pivots, log_ref)


def second_kernel(
    scale, near_refs, far_refs, x_refs, first_ref, first_log, out_ref, log_ref,
    work, cross, mine, logs, pivots, near_part, far_part,
):
    me = lax.axis_index("tangent")
    shards = len(x_refs)
    inner = shards // 2
    bc = out_ref.shape[1]
    full = work.shape[0]
    top = pl.multiple_of((me & (inner - 1)) * bc, BLOCK)
    rows = pl.ds(top, bc)

    @pl.when(me < inner)
    def _():
        mine[:, 0:full] = first_ref[rows, :]
        mine[:, full:] = jnp.zeros((bc, full), F32)
        log_ref[...] = first_log[:, rows]

    @pl.when(me >= inner)
    def _():
        for k in range(inner):
            collect(far_refs[k], scale, far_part)
            cols = pl.ds(pl.multiple_of((me ^ k) * bc - full, BLOCK), bc)
            for j in range(inner):
                place = pl.ds(pl.multiple_of((me ^ k ^ (j + inner)) * bc, BLOCK), bc)
                cross[place, cols] = far_part[j * bc : (j + 1) * bc, :]
            collect(near_refs[k], scale, near_part)
            near_blocks((me ^ k) & (inner - 1), near_part, work)
        cross[...] = three_pass(first_ref[...], cross[...], 1)
        work[...] = work[...] - three_pass(cross[...], cross[...], 0)
        eliminate(full // BLOCK, work, pivots)
        log_rows(pivots, logs)
        row_block = (lax.broadcasted_iota(jnp.int32, (bc, full), 0) + top) // BLOCK
        col_block = lax.broadcasted_iota(jnp.int32, (bc, full), 1) // BLOCK
        own = jnp.where(row_block >= col_block, work[rows, :], 0.0)
        mine[:, full:] = own
        mine[:, 0:full] = -three_pass(three_pass(own, cross[...].T, 1), first_ref[...], 1)
        log_ref[...] = logs[:, rows]

    def times(x_ref, peer):
        high, low = two_parts(mine[:, pl.ds(pl.multiple_of(peer * bc, BLOCK), bc)])
        return matmul(x_ref[...], high, ((1,), (1,))) + matmul(x_ref[...], low, ((1,), (1,)))

    out_ref[...] = times(x_refs[0], me)
    for k in range(1, shards):
        peer = me ^ k

        @pl.when(peer < me)
        def _():
            out_ref[...] += times(x_refs[k], peer)


def call(kernel, counts, out_shapes, scratch, operands, cost=None, after=()):
    inputs, waits = len(operands), len(after)

    def unpacked(*refs):
        refs = refs[:inputs] + refs[inputs + waits :]
        groups, at = [], 0
        for count in counts:
            groups.append(refs[at : at + count])
            at += count
        kernel(*groups, *refs[at:])

    return pl.pallas_call(
        unpacked,
        out_shape=out_shapes,
        in_specs=[pl.BlockSpec(memory_space=pltpu.VMEM)] * inputs + [pl.BlockSpec(memory_space=pl.ANY)] * waits,
        scratch_shapes=scratch,
        cost_estimate=cost,
        compiler_params=pltpu.CompilerParams(vmem_limit_bytes=48 * 1024 * 1024),
    )(*operands, *after)


def flip(array, axis, bit):
    return lax.ppermute(array, axis, [(i, i ^ bit) for i in range(lax.axis_size(axis))])


def flips(blocks, bits):
    for bit in bits:
        blocks = {**blocks, **{k ^ bit: flip(v, "tangent", bit) for k, v in blocks.items()}}
    return blocks


def around_space(arrays):
    count = lax.axis_size("space")
    return [lax.ppermute(v, "space", [(i, (i + k) % count) for i in range(count)]) for k, v in enumerate(arrays, 1)]


def added(arrived, after=()):
    shape = jax.ShapeDtypeStruct(arrived[0].shape, F32)
    return call(sum_kernel, (len(arrived),), shape, [], arrived, after=after)


def orthonormalize(x):
    shards, count = lax.axis_size("tangent"), lax.axis_size("space")
    rows, bc = x.shape
    half, inner = bc // 2, shards // 2
    direct = count <= 8
    cuts = count if direct else 1
    bits = [1 << b for b in reversed(range(inner.bit_length() - 1))]
    scale = 1.0 / (float(rows) * count)
    near_rows, far_rows = half + half // 2 + (inner - 1) * half, inner * bc

    def dealt(held):
        return (jax.ShapeDtypeStruct((held // cuts, bc), F32),) * cuts

    def spread_out(parts):
        if not direct:
            return [lax.psum(parts[0], "space")]
        return [parts[0]] + around_space(parts[1:])

    far_own = flip(x, "tangent", inner)
    near_x = flips({0: x}, bits)
    near_x = [near_x[k] for k in range(inner)]
    near = call(near_gram_kernel, (inner, cuts), dealt(near_rows), [pltpu.VMEM((near_rows, bc), F32)], near_x)
    near_sum = added(spread_out(near))
    around = [near_sum] + around_space([near_sum] * (cuts - 1))
    far_x = flips({0: lax.optimization_barrier((far_own, near_sum))[0]}, bits)
    far_x = [far_x[k] for k in range(inner)]
    far = call(far_gram_kernel, (1, inner, cuts), dealt(far_rows), [pltpu.VMEM((far_rows, bc), F32)], [x] + far_x)
    arrived = spread_out(far)
    near = jnp.stack(lax.optimization_barrier((around, far[0]))[0])
    far_sum = added(arrived, after=[near])
    far_around = [far_sum] + around_space([far_sum] * (cuts - 1))
    near = flips({0: near}, [inner])
    near[inner] = lax.optimization_barrier((near[inner], far_sum))[0]
    near = flips(near, bits)
    near = [near[k] for k in range(shards)]
    full = inner * bc
    square, column = pltpu.VMEM((full, full), F32), pltpu.VMEM((full, BLOCK), F32)
    near_part = pltpu.VMEM((near_rows, bc), F32)
    first, first_log = call(
        lambda *refs: first_kernel(scale, *refs),
        (shards,),
        (jax.ShapeDtypeStruct((full, full), F32), jax.ShapeDtypeStruct((1, full), F32)),
        [column, near_part],
        near,
        cost=pl.CostEstimate(flops=16 * 10**9, bytes_accessed=4 * 10**6, transcendentals=0),
    )
    far_around = lax.optimization_barrier((far_around, first_log))[0]
    late = flips({0: jnp.stack(far_around)}, bits)
    late = [late[k] for k in range(inner)]
    out, logs = call(
        lambda *refs: second_kernel(scale, *refs),
        (inner, inner, shards),
        (jax.ShapeDtypeStruct((rows, bc), F32), jax.ShapeDtypeStruct((1, bc), F32)),
        [
            square, square, pltpu.VMEM((bc, 2 * full), F32), pltpu.VMEM((1, full), F32),
            column, near_part, pltpu.VMEM((far_rows, bc), F32),
        ],
        near[:inner] + late + near_x + far_x + [first, first_log],
    )
    return out, logs[0]


def site_rows(x, y, tall):
    column = jnp.concatenate([row.astype(jnp.int32) for row in x], axis=1)
    row = jnp.concatenate([v.astype(jnp.int32) + c * TALL for c, v in enumerate(y)], axis=1)
    return column, row


def one_hot(rows, index):
    return jnp.where(lax.broadcasted_iota(jnp.int32, (rows, index.shape[1]), 0) == index, 1.0, 0.0)


def own_sites(position_ref):
    cells = position_ref.shape[0]
    x, y = [[position_ref[c, i : i + 1, :] for c in range(cells)] for i in range(2)]
    return site_rows(x, y, cells * TALL)


def placement(position_ref):
    tall = position_ref.shape[0] * TALL
    column, row = own_sites(position_ref)
    return one_hot(WIDE * tall, column * tall + row).astype(BF16)


def three_parts(a):
    high, rest = a.astype(BF16), None
    rest = a - high.astype(F32)
    mid = rest.astype(BF16)
    return high, mid, (rest - mid.astype(F32)).astype(BF16)


def sort_kernel(position_ref, momentum_ref, count_ref, tangent_ref, state_ref, left_ref, right_ref, raw):
    cells, comps, slots, bc = tangent_ref.shape
    high = cells * TALL
    place = placement(position_ref)
    raw[...] = jnp.zeros(raw.shape, F32)
    lane = lax.broadcasted_iota(jnp.int32, (1, slots), 1)
    for c in range(cells):
        alive = jnp.where(lane < count_ref[c], 1.0, 0.0)
        rows = [position_ref[c, 0:1, :], position_ref[c, 1:2, :], momentum_ref[c, 0:1, :], momentum_ref[c, 1:2, :], alive]
        for item, row in enumerate(rows):
            for p, part in enumerate(three_parts(row)):
                at = ITEMS * (p * cells + c) + item
                raw[at : at + 1, :] = part.astype(F32)
    for ref in (left_ref, right_ref):
        ref[10] = jnp.zeros((high, bc), BF16)
        ref[10, :, 0:slots] = raw[...].astype(BF16)
    slot = lax.broadcasted_iota(jnp.int32, (slots, bc), 0)
    for comp in range(comps):
        rows = [jnp.where(slot < count_ref[c], tangent_ref[c, comp], 0.0) for c in range(cells)]
        top, low = two_parts(jnp.concatenate(rows, axis=0))
        moved = matmul(place, top, ((1,), (0,))) + matmul(place, low, ((1,), (0,)))
        state_ref[comp] = moved.reshape(WIDE, high, bc)
        near = moved.astype(BF16).reshape(WIDE, high, bc)
        if comp < 2:
            left_ref[3 * comp : 3 * comp + 3] = near[0:3]
            right_ref[3 * comp : 3 * comp + 3] = near[WIDE - 3 :]
        else:
            at = 6 + 2 * (comp - 2)
            left_ref[at : at + 2] = near[0:2]
            right_ref[at : at + 2] = near[WIDE - 2 :]


def bond(far_x, far_y, own_x, own_y, both, shift_x, shift_y):
    dx = shift_x + far_x - own_x
    dy = shift_y + far_y - own_y
    dist2 = dx * dx + dy * dy
    within = jnp.logical_and(dist2 < CUT2, both > 0.5)
    weight = jnp.where(within, 1.0, 0.0)
    safe = jnp.where(within, dist2, CUT2)
    inverse = 1.0 / safe
    inv_three = inverse * inverse * inverse
    inv_six = inv_three * inv_three
    energy = 4.0 * (inv_six - inv_three) + 1.0
    energy_1 = 4.0 * (3.0 * inv_three - 6.0 * inv_six) * inverse
    energy_2 = 4.0 * (42.0 * inv_six - 12.0 * inv_three) * inverse * inverse
    taper = 1.0 - safe * (1.0 / CUT2)
    switch = taper * taper
    switch_1 = taper * (-2.0 / CUT2)
    switch_2 = 2.0 / (CUT2 * CUT2)
    twice_1 = (energy_1 * switch + energy * switch_1) * weight * 2.0
    four_2 = (energy_2 * switch + 2.0 * energy_1 * switch_1 + energy * switch_2) * weight * 4.0
    k_xx = twice_1 + four_2 * dx * dx
    k_xy = four_2 * dx * dy
    k_yy = twice_1 + four_2 * dy * dy
    return twice_1 * dx, twice_1 * dy, (k_xx, k_xy, k_yy)


def up(a):
    return pltpu.roll(a, a.shape[0] - 1, 0)


def down(a):
    return pltpu.roll(a, 1, 0)


KICKS = tuple((0.5 if step in (0, STEPS) else 1.0) * DT for step in range(STEPS + 1))


def on_lattice(cells, tall, rows, offset):
    x, y = [[sum(part[c] for part in rows[i]) for c in range(cells)] for i in range(2)]
    column, row = site_rows(x, y, tall)
    stands = one_hot(tall, row)
    flat = [jnp.concatenate(part, axis=1) for item in rows for part in item]
    left = jnp.concatenate([stands * v for v in flat], axis=0).astype(BF16)
    spread_values = matmul(left, one_hot(BLOCK, column + offset).astype(BF16), ((1,), (1,)))
    out, at = [], 0
    for item in rows:
        parts = [spread_values[(at + p) * tall : (at + p + 1) * tall] for p in range(len(item))]
        out.append(sum(parts[1:], parts[0]))
        at += len(item)
    return out


def motion_kernel(
    position_ref, momentum_ref, count_ref, state_ref, low_ref, high_ref, phase_ref, x_ref, wide, bonds
):
    cells, comps, slots, bc = x_ref.shape
    tall = cells * TALL
    halo = STEPS + 1
    columns = WIDE + 2 * halo
    for comp in range(comps):
        wide[comp, halo : halo + WIDE] = state_ref[comp]
        if comp < 2:
            wide[comp, 0:halo] = low_ref[3 * comp : 3 * comp + 3].astype(F32)
            wide[comp, halo + WIDE :] = high_ref[3 * comp : 3 * comp + 3].astype(F32)
        else:
            at = 6 + 2 * (comp - 2)
            wide[comp, 1:halo] = low_ref[at : at + 2].astype(F32)
            wide[comp, halo + WIDE : columns - 1] = high_ref[at : at + 2].astype(F32)
    slot = lax.broadcasted_iota(jnp.int32, (1, slots), 1)
    own = [
        [[part.astype(F32) for part in three_parts(ref[c, i : i + 1, :])] for c in range(cells)]
        for ref in (position_ref, momentum_ref)
        for i in range(2)
    ]
    own = [[[cell[p] for cell in item] for p in range(3)] for item in own]
    own.append([[jnp.where(slot < count_ref[c], 1.0, 0.0) for c in range(cells)]])
    slabs = [on_lattice(cells, tall, own, halo)]
    for ref, offset in ((low_ref, halo - WIDE), (high_ref, halo + WIDE)):
        sent = ref[10, :, 0:slots].astype(F32)

        def row(item, p, c):
            at = ITEMS * (p * cells + c) + item
            return sent[at : at + 1, :]

        rows = [[[row(i, p, c) for c in range(cells)] for p in range(3 if i < 4 else 1)] for i in range(ITEMS)]
        slabs.append(on_lattice(cells, tall, rows, offset))
    x, y, speed_x, speed_y, alive = [a + b + c for a, b, c in zip(*slabs)]
    site = lax.broadcasted_iota(jnp.int32, (tall, BLOCK), 0)
    lane = lax.broadcasted_iota(jnp.int32, (tall, BLOCK), 1)
    shift_y = jnp.where(lax.rem(site, TALL) == TALL - 1, float(TALL), 0.0)
    shift_x = jnp.where(jnp.logical_or(lane == halo - 1, lane == halo + WIDE - 1), float(WIDE), 0.0)

    def right(a):
        return pltpu.roll(a, BLOCK - 1, 1)

    def left(a):
        return pltpu.roll(a, 1, 1)

    beside, over = alive * right(alive), alive * up(alive)
    for step, kick in enumerate(KICKS):
        side_x, side_y, k_side = bond(right(x), right(y), x, y, beside, shift_x, 0.0)
        over_x, over_y, k_over = bond(up(x), up(y), x, y, over, 0.0, shift_y)
        for a, k in enumerate(k_side + k_over):
            bonds[step, a] = k.astype(BF16).astype(F32)
        speed_x = speed_x + kick * (side_x - left(side_x) + over_x - down(over_x))
        speed_y = speed_y + kick * (side_y - left(side_y) + over_y - down(over_y))
        if step < STEPS:
            x, y = x + DT * speed_x, y + DT * speed_y
    column, row = own_sites(position_ref)
    picks = one_hot(BLOCK, column + halo).astype(BF16)
    stands = one_hot(tall, row)
    for item, value in enumerate((x, y, speed_x, speed_y)):
        back = sum(matmul(part, picks, ((1,), (0,))) for part in three_parts(value))
        back = jnp.sum(jnp.where(stands > 0.5, back, 0.0), axis=0, keepdims=True)
        for c in range(cells):
            phase_ref[c, item : item + 1, :] = back[:, c * slots : (c + 1) * slots]

    def rounded(comp, c):
        return wide[comp, c].astype(BF16).astype(F32)

    for step, kick in enumerate(KICKS):

        def push(c, k0, e_x, e_y):
            k_xx, k_xy, k_yy = [
                jnp.broadcast_to(bonds[step, k0 + a][:, c : c + 1], (tall, bc)) for a in range(3)
            ]
            return k_xx * e_x + k_xy * e_y, k_xy * e_x + k_yy * e_y

        low_x, low_y = rounded(0, step), rounded(1, step)
        next_x, next_y = rounded(0, step + 1), rounded(1, step + 1)
        pull_x, pull_y = push(step, 0, next_x - low_x, next_y - low_y)
        for c in range(step + 1, columns - 1 - step):
            low_x, low_y = next_x, next_y
            next_x, next_y = rounded(0, c + 1), rounded(1, c + 1)
            side_x, side_y = push(c, 0, next_x - low_x, next_y - low_y)
            over_x, over_y = push(c, 3, up(low_x) - low_x, up(low_y) - low_y)
            rate_x = wide[2, c] + kick * (side_x - pull_x + over_x - down(over_x))
            rate_y = wide[3, c] + kick * (side_y - pull_y + over_y - down(over_y))
            wide[2, c], wide[3, c] = rate_x, rate_y
            if step < STEPS:
                wide[0, c] = wide[0, c] + DT * rate_x
                wide[1, c] = wide[1, c] + DT * rate_y
            pull_x, pull_y = side_x, side_y
    place = placement(position_ref)
    for comp in range(comps):
        value = wide[comp, halo : halo + WIDE].reshape(WIDE * tall, bc).astype(BF16)
        back = matmul(place, value, ((0,), (0,))).astype(BF16)
        for c in range(cells):
            x_ref[c, comp] = back[c * slots : (c + 1) * slots]


def dynamics(positions, momenta, cell_count, tangent):
    cells, comps, slots, bc = tangent.shape
    tall = cells * TALL
    columns = WIDE + 2 * (STEPS + 1)
    count = lax.axis_size("space")
    forward = [(i, (i + 1) % count) for i in range(count)]
    backward = [(b, a) for a, b in forward]
    halo = jax.ShapeDtypeStruct((11, tall, bc), BF16)
    vmem, smem = pl.BlockSpec(memory_space=pltpu.VMEM), pl.BlockSpec(memory_space=pltpu.SMEM)
    params = pltpu.CompilerParams(vmem_limit_bytes=48 * 1024 * 1024)
    state, left, right = pl.pallas_call(
        sort_kernel,
        out_shape=(jax.ShapeDtypeStruct((comps, WIDE, tall, bc), F32), halo, halo),
        in_specs=[vmem, vmem, smem, vmem],
        scratch_shapes=[pltpu.VMEM((tall, slots), F32)],
        compiler_params=params,
    )(positions, momenta, cell_count, tangent)
    low, high = lax.ppermute(right, "space", forward), lax.ppermute(left, "space", backward)
    return pl.pallas_call(
        motion_kernel,
        out_shape=(jax.ShapeDtypeStruct((cells, 4, slots), F32), jax.ShapeDtypeStruct(tangent.shape, BF16)),
        in_specs=[vmem, vmem, smem, vmem, vmem, vmem],
        scratch_shapes=[
            pltpu.VMEM((comps, columns, tall, bc), F32),
            pltpu.VMEM((STEPS + 1, 6, tall, BLOCK), F32),
        ],
        compiler_params=params,
    )(positions, momenta, cell_count, state, low, high)


def body(positions, momenta, cell_count, tangent):
    phase, x = dynamics(positions, momenta, cell_count, tangent)
    out, stretch = orthonormalize(x.reshape(-1, x.shape[3]))
    return (phase, out.reshape(x.shape), stretch)


def solution(mesh):
    placed = (
        P(("groups", "space"), None, None),
        P(("groups", "space"), None, None),
        P(("groups", "space")),
        P(("groups", "space"), None, None, "tangent"),
    )
    return jax.shard_map(
        body,
        mesh=mesh,
        in_specs=placed,
        out_specs=(
            P(("groups", "space"), None, None),
            P(("groups", "space"), None, None, "tangent"),
            P(("groups", "tangent")),
        ),
        check_vma=False,
    )
```
